256 devices in a mesh: row: 16 (over z, y_lo), col: 16 (over y_hi, x, core).
Axes of the slice: x: 4, y: 4 (y_hi: 2, y_lo: 2; y = y_hi * 2 + y_lo), z: 8, core: 2. Of those that a mesh axis runs over, the one named last changes fastest.
Arguments:
- paths_in: float32 [32768, 256], P(('row', 'col')), may hold values from 0.05 to 4
- dep_in: float32 [32768, 256], P(('row', 'col')), may hold values from 0 to 4
- levels: int32 [32768, 256], P(('row', 'col')), may hold values from 0 to 4, as said below
- tile_src: int32 [16, 16, 16, 4], P('row', 'col'), may hold values from 0 to 15, as said below
- pattern: int32 [16, 16, 16, 4, 128, 128], P('row', 'col'), may hold values from 0 to 1, as said below
Outputs:
- dependency: float32 [32768, 256], P(('row', 'col'))
The draws below stay inside these ranges and needn't reach their ends.
Inputs may be any that keep to these rules, and one draw needn't show every extreme that they name: The value 4 marks a vertex outside the window's levels for that source. A program may send only the non-zero entries of a level's rounded path counts or backward weights, together with their positions, in any encoding that loses nothing. `tile_src`: within one device the 4 source tiles of a destination tile row are distinct, and every source tile index appears in exactly 4 of the device's slots. `pattern`: each slot holds either an all-zero tile or a tile of independent 0/1 entries; a device has from 1 to 64 nonzero tiles, and some device has all its slots nonzero.
All inputs are finite; a program needn't handle non-finite values.
Results may differ from the reference program's by a relative error of at most 0.0016.
Values may be sent and summed in bfloat16 or wider, within the bound.
A program may use at most 64 MiB of HBM per device.

```python
import math
import jax
import jax.numpy as jnp
from jax import lax

VERT_DEV = 128
SOURCES = 256
TILE = 128
BAND = 4
ROW_BLOCKS = 16
COL_BLOCKS = 16
DEST_TILES = 16
SRC_TILES = 16
VERTICES = 32768
N_ROW = 16
N_COL = 16


def band_sources(device_key):
    key_perm, key_shift = jax.random.split(device_key)
    source_perm = jax.random.permutation(key_perm, SRC_TILES)
    row_shift = jax.random.permutation(key_shift, DEST_TILES)
    slots = (row_shift[:, None] + jnp.arange(BAND)[None, :]) % SRC_TILES
    return source_perm[slots].astype(jnp.int32)


def draw_tile_src(key, part):
    device_keys = jax.random.split(jax.random.fold_in(key, 11), ROW_BLOCKS * COL_BLOCKS)
    chosen = jax.vmap(band_sources)(device_keys)
    return chosen.reshape(ROW_BLOCKS, COL_BLOCKS, DEST_TILES, BAND)


def shuffled(rank_key):
    return jax.random.permutation(rank_key, DEST_TILES * BAND)


def draw_pattern(key, part):
    devices = ROW_BLOCKS * COL_BLOCKS
    slots = DEST_TILES * BAND
    key_count, key_top, key_rank, key_bits = jax.random.split(jax.random.fold_in(key, 23), 4)
    raw_draw = jax.random.randint(key_count, (devices,), 1, slots + 1)
    live_count = jnp.maximum(raw_draw * raw_draw // slots, 1)
    busiest = jax.random.randint(key_top, (), 0, devices)
    live_count = jnp.where(jnp.arange(devices) == busiest, slots, live_count)
    slot_rank = jax.vmap(shuffled)(jax.random.split(key_rank, devices))
    live_slots = slot_rank < live_count[:, None]
    entries = jax.random.randint(key_bits, (devices, slots, TILE, TILE), 0, 8) == 0
    values = jnp.logical_and(entries, live_slots[:, :, None, None]).astype(jnp.int32)
    return values.reshape(ROW_BLOCKS, COL_BLOCKS, DEST_TILES, BAND, TILE, TILE)


def draw_levels(key, part):
    key_order, key_ticket = jax.random.split(jax.random.fold_in(key, 37))
    source_order = jax.random.permutation(key_order, SOURCES).astype(jnp.int32)
    exponent = source_order * 8 // SOURCES
    ticket = jax.random.randint(key_ticket, (VERTICES, SOURCES), 0, 1024)
    bound_sum = jnp.zeros_like(exponent)
    level_value = jnp.zeros((VERTICES, SOURCES), jnp.int32)
    for section in range(4):
        one_share = jnp.minimum(jnp.left_shift(jnp.ones_like(exponent), exponent + 2 * section), 205)
        bound_sum = bound_sum + one_share
        level_value = level_value + (ticket >= bound_sum[None, :]).astype(jnp.int32)
    return level_value


def block_levels(rng, shape, pieces, low, largest):
    def one(position, shards_of):
        steps = jax.random.uniform(jax.random.fold_in(jax.random.fold_in(rng, 6), position), (shards_of,), jnp.float32, low / len(pieces), largest / len(pieces))
        return jnp.repeat(jnp.exp(steps), shape[position] // shards_of).reshape((-1,) + (1,) * (len(shape) - position - 1))

    factor_of = one(*pieces[0])
    for cut in pieces[1:]:
        factor_of = factor_of * one(*cut)
    return factor_of


def setup_inputs(seed: int = 0) -> dict:
    keys = jax.random.split(jax.random.key(seed), 6)
    paths_in = jnp.clip(jnp.exp(math.log(4.0) - 4.3820266 * jax.random.uniform(keys[0], (VERTICES, SOURCES), jnp.float32) ** block_levels(keys[0], (VERTICES, SOURCES), ((0, 256),), -0.2, 0.2)), 0.05, 4.0)
    dep_in = jnp.clip(4.0 * jax.random.uniform(keys[1], (VERTICES, SOURCES), jnp.float32) ** block_levels(keys[1], (VERTICES, SOURCES), ((0, 256),), -0.2, 0.2), 0.0, 4.0)
    levels = draw_levels(jax.random.fold_in(keys[5], 71), 0)
    tile_src = draw_tile_src(jax.random.fold_in(keys[5], 71), 0)
    pattern = draw_pattern(jax.random.fold_in(keys[5], 71), 0)
    return dict(paths_in=paths_in, dep_in=dep_in, levels=levels, tile_src=tile_src, pattern=pattern)


def rounded(values):
    return lax.optimization_barrier(values.astype(jnp.bfloat16)).astype(jnp.float32)


def forward_apply(frontier, tile_src, pattern):
    vtiles = VERT_DEV // TILE
    blocked = frontier.reshape(N_ROW, N_COL * VERT_DEV, SOURCES)
    summed = jnp.zeros((N_ROW, N_COL, VERT_DEV, SOURCES), jnp.float32)

    def visit(device, summed):
        row_block = (device // N_COL).astype(jnp.int32)
        col_block = (device % N_COL).astype(jnp.int32)
        anchor = jnp.zeros((), jnp.int32)
        source_block = lax.dynamic_index_in_dim(blocked, row_block, 0, keepdims=False)
        source_block = source_block.reshape(N_COL * vtiles, TILE, SOURCES)
        source_ids = tile_src[row_block, col_block]
        tile_values = pattern[row_block, col_block].astype(jnp.float32)
        picked = source_block[source_ids]
        product = jnp.einsum("ibrj,ibjs->irs", tile_values, picked, precision=lax.Precision.HIGHEST)
        product = product.reshape(N_ROW, 1, VERT_DEV, SOURCES)
        current = lax.dynamic_slice(summed, (anchor, col_block, anchor, anchor), (N_ROW, 1, VERT_DEV, SOURCES))
        return lax.dynamic_update_slice(summed, current + product, (anchor, col_block, anchor, anchor))

    summed = lax.fori_loop(jnp.int32(0), jnp.int32(N_ROW * N_COL), visit, summed)
    return summed.reshape(N_ROW * N_COL * VERT_DEV, SOURCES)


def backward_apply(weight, tile_src, pattern):
    vtiles = VERT_DEV // TILE
    src_count = N_COL * vtiles
    blocked = weight.reshape(N_ROW, N_COL, VERT_DEV, SOURCES)
    summed = jnp.zeros((N_ROW, N_COL * VERT_DEV, SOURCES), jnp.float32)

    def visit(device, summed):
        row_block = (device // N_COL).astype(jnp.int32)
        col_block = (device % N_COL).astype(jnp.int32)
        anchor = jnp.zeros((), jnp.int32)
        dest_block = lax.dynamic_index_in_dim(blocked, col_block, 1, keepdims=False)
        dest_block = dest_block.reshape(N_ROW * vtiles, TILE, SOURCES)
        source_ids = tile_src[row_block, col_block]
        tile_values = pattern[row_block, col_block].astype(jnp.float32)
        spread = jnp.einsum("ibrj,irs->ibjs", tile_values, dest_block, precision=lax.Precision.HIGHEST)
        select = (source_ids[:, :, None] == jnp.arange(src_count, dtype=jnp.int32)[None, None, :]).astype(jnp.float32)
        product = jnp.einsum("ibt,ibjs->tjs", select, spread, precision=lax.Precision.HIGHEST)
        product = product.reshape(1, N_COL * VERT_DEV, SOURCES)
        current = lax.dynamic_slice(summed, (row_block, anchor, anchor), (1, N_COL * VERT_DEV, SOURCES))
        return lax.dynamic_update_slice(summed, current + product, (row_block, anchor, anchor))

    summed = lax.fori_loop(jnp.int32(0), jnp.int32(N_ROW * N_COL), visit, summed)
    return summed.reshape(N_ROW * N_COL * VERT_DEV, SOURCES)


def reference(paths_in, dep_in, levels, tile_src, pattern):
    level_masks = [(levels == distance).astype(jnp.float32) for distance in range(4)]
    path_counts = [level_masks[0] * paths_in]
    for distance in range(1, 4):
        frontier = rounded(path_counts[-1])
        path_counts.append(level_masks[distance] * forward_apply(frontier, tile_src, pattern))
    weight = rounded(level_masks[3] * (1.0 + dep_in) / jnp.maximum(path_counts[3], 1.0))
    dependency = jnp.zeros(paths_in.shape, jnp.float32)
    for distance in (2, 1, 0):
        dependence = level_masks[distance] * path_counts[distance] * backward_apply(weight, tile_src, pattern)
        dependency = dependency + dependence
        if distance > 0:
            weight = rounded(level_masks[distance] * (1.0 + dependence) / jnp.maximum(path_counts[distance], 1.0))
    return dependency
```

```python
import functools

import jax
import jax.numpy as jnp
from jax import lax
from jax.experimental import pallas as pl
from jax.experimental.pallas import tpu as pltpu
from jax.sharding import PartitionSpec as P

MESH = pl.DeviceIdType.MESH
F32, BF16, I16, I32 = jnp.float32, jnp.bfloat16, jnp.int16, jnp.int32

ZS, XS, HI = 8, 4, 2
LVLS = 3
FWD = (-5.0, 1365.0)
BWD = (-44.0, 744.0)
LN2 = 0.6931471805599453
COL_STEPS = [(2, 1), (1, 1), (3, 1), (0, 1), (2, 0), (1, 0), (3, 0)]


def encode(x, code):
    low, steps = code
    v = jnp.log(jnp.maximum(x, 2.0**low)) * (steps / LN2) + (0.5 - low * steps)
    return (v.astype(I32) - 32768).astype(I16)


def decode(c, code):
    low, steps = code
    v = c.astype(I32).astype(F32)
    x = jnp.exp(v * (LN2 / steps) + (32768.0 / steps + low) * LN2)
    return jnp.where(v > -32768.0, x, 0.0)


def kernel(
    tsrc, bslot, paths_in, dep_in, levels, pattern, out,
    stage, acat, at, gath, wgt, local, part, paths, total,
    ysend, yrecv, qsend, qrecv, psend, precv, fsend, frecv,
    csend, crecv, isend, irecv,
    load_sem,
    ag_s, ag_r, sib_s, sib_r,
    y_s, y_r, q_s, q_r, p_s, p_r, f_s, f_r,
    wy_s, wy_r, wb_s, wb_r, wq_s, wq_r, wp_s, wp_r,
    c_s, c_r, i_s, i_r,
):
    r, c = lax.axis_index("row"), lax.axis_index("col")
    z, y = r // 2, r % 2
    chip, core = c // 2, c % 2
    yhi, x = chip // XS, chip % XS
    s = 1 - 2 * core
    half = 64

    def row_dev(zz, yy):
        return {"row": zz * 2 + yy, "col": c}

    def ring(off):
        return (z + s * off + 2 * ZS) % ZS

    ahead, behind = row_dev(ring(1), y), row_dev(ring(-1), y)
    across = row_dev(z, 1 - y)
    sibling = {"row": r, "col": chip * 2 + 1 - core}

    def chip_at(n, sign=1):
        dx, dy = COL_STEPS[n]
        return ((yhi + dy) % HI) * XS + (x + sign * dx + XS) % XS

    def col_dev(n):
        return {"row": r, "col": chip_at(n) * 2 + core}

    def move(src, dst, ssem, rsem, dev):
        return pltpu.make_async_remote_copy(
            src_ref=src, dst_ref=dst, send_sem=ssem, recv_sem=rsem, device_id=dev, device_id_type=MESH
        )

    def load(i):
        return pltpu.make_async_copy(pattern.at[pl.ds(i * 4, 4)], stage.at[i], load_sem.at[i])

    for i in range(16):
        load(i).start()

    barrier = pltpu.get_barrier_semaphore()
    partners = [ahead, behind, across, sibling] + [col_dev(n) for n in range(7)]
    for dev in partners:
        pl.semaphore_signal(barrier, inc=1, device_id=dev, device_id_type=MESH)
    pl.semaphore_wait(barrier, len(partners))

    def gather_col_start(lvl):
        own = gath.at[lvl, c]
        for n in range(7):
            move(own, own, ag_s.at[n], ag_r.at[lvl, n], col_dev(n)).start()
        move(own, own, sib_s.at[7], sib_r.at[lvl, 7], sibling).start()

    def gather_col_end(lvl):
        own = gath.at[lvl, c]
        for n in (5, 6, 4, 3, 1, 2, 0):
            got = gath.at[lvl, chip_at(n, -1) * 2 + core]
            move(got, got, ag_s.at[n], ag_r.at[lvl, n], col_dev(n)).wait_recv()
            move(got, got, sib_s.at[n], sib_r.at[lvl, n], sibling).start()
        for n in range(7):
            move(own, own, ag_s.at[n], ag_r.at[lvl, n], col_dev(n)).wait_send()
        for n in range(8):
            move(own, own, sib_s.at[n], sib_r.at[lvl, n], sibling).wait()

    def zoff(j):
        return jnp.where(j % 2 == 0, 4 - j // 2, (j - 7) // 2)

    def forward_tile(i):
        rhs = jnp.concatenate([local[tsrc[i * 4 + e]] for e in range(4)], axis=0)
        part[i] = jnp.dot(acat[i], rhs, preferred_element_type=F32)

    def y_move(lvl, j):
        return move(ysend.at[j], yrecv.at[lvl, j], y_s.at[j], y_r.at[lvl, j], across)

    def q_move(lvl, m, dev):
        return move(qsend.at[m], qrecv.at[lvl, m], q_s.at[m], q_r.at[lvl, m], dev)

    def p_move(lvl, m, dev):
        return move(psend.at[m], precv.at[lvl, m], p_s.at[m], p_r.at[lvl, m], dev)

    def forward_pair(lvl, j):
        zd = ring(zoff(j))

        @pl.loop(0, 2)
        def _(t):
            forward_tile(zd * 2 + t)

        ysend[j] = encode(part[zd * 2 + 1 - y, :half], FWD)
        y_move(lvl, j).start()

    def q_sum(lvl, j, got):
        zd = ring(zoff(j))
        for t in range(2):
            v = part[zd * 2 + t, half:]
            for m in got:
                v += decode(qrecv[lvl, m, t], FWD)
            yield t, v

    def p_sum(lvl, j, got):
        y_move(lvl, j).wait_recv()
        v = part[ring(zoff(j)) * 2 + y, :half] + decode(yrecv[lvl, j], FWD)
        for m in got:
            v += decode(precv[lvl, m], FWD)
        return v

    def hop(m):
        return (2 * m, ahead) if m < 4 else (2 * (m - 4) + 1, behind)

    def q_step(lvl, m):
        j, dev = hop(m)
        got = [] if m in (0, 4) else [m - 1]
        for g in got:
            q_move(lvl, g, dev).wait_recv()
        for t, v in q_sum(lvl, j, got):
            qsend[m, t] = encode(v, FWD)
        q_move(lvl, m, dev).start()

    def p_step(lvl, m):
        j, dev = hop(m)
        got = [] if m in (0, 4) else [m - 1]
        for g in got:
            p_move(lvl, g, dev).wait_recv()
        psend[m] = encode(p_sum(lvl, j, got), FWD)
        p_move(lvl, m, dev).start()

    def f_move(lvl):
        return move(fsend, frecv.at[lvl], f_s, f_r.at[lvl], across)

    def sum_row(lvl):
        @pl.loop(0, 2)
        def _(j):
            forward_pair(lvl, j)

        q_step(lvl, 0)
        q_step(lvl, 4)

        @pl.loop(2, 4)
        def _(j):
            forward_pair(lvl, j)

        p_step(lvl, 0)
        p_step(lvl, 4)

        @pl.loop(4, 8)
        def _(j):
            forward_pair(lvl, j)

        for m in (1, 5, 2, 6, 3):
            q_step(lvl, m)
            p_step(lvl, m)
        for m in (3, 6):
            q_move(lvl, m, ahead).wait_recv()
        for t, v in q_sum(lvl, 7, [3, 6]):
            part[z * 2 + t, half:] = v
        fsend[...] = encode(part[z * 2 + 1 - y, half:], FWD)
        f_move(lvl).start()
        for m in (3, 6):
            p_move(lvl, m, ahead).wait_recv()
        total[:half] = p_sum(lvl, 7, [3, 6])
        f_move(lvl).wait()
        total[half:] = part[z * 2 + y, half:] + decode(frecv[lvl], FWD)
        for j in range(8):
            y_move(lvl, j).wait_send()
        for m in range(7):
            q_move(lvl, m, ahead).wait_send()
            p_move(lvl, m, ahead).wait_send()

    def came_from(m):
        return ring(-(m + 1)) if m < 4 else ring(m - 3)

    def wb_move(lvl, zz, m, dev):
        ref = wgt.at[lvl, zz * 2 + y]
        return move(ref, ref, wb_s.at[m], wb_r.at[lvl, m], dev)

    def wq_move(lvl, zz, m, dev):
        ref = wgt.at[lvl, zz * 2 + 1 - y, pl.ds(half, half)]
        return move(ref, ref, wq_s.at[m], wq_r.at[lvl, m], dev)

    def wp_move(lvl, zz, m):
        ref = wgt.at[lvl, zz * 2 + y, pl.ds(0, half)]
        return move(ref, ref, wp_s.at[m], wp_r.at[lvl, m], across)

    def wy_move(lvl):
        ref = wgt.at[lvl, r]
        return move(ref, ref, wy_s, wy_r.at[lvl], across)

    def gather_row(lvl):
        wy_move(lvl).start()
        wb_move(lvl, z, 0, ahead).start()
        wb_move(lvl, z, 4, behind).start()
        wy_move(lvl).wait_recv()
        wq_move(lvl, z, 0, ahead).start()
        wq_move(lvl, z, 4, behind).start()
        for m in (0, 4, 1, 5, 2, 6, 3):
            dev = ahead if m < 4 else behind
            zz = came_from(m)
            wb_move(lvl, zz, m, dev).wait_recv()
            if m not in (3, 6):
                wb_move(lvl, zz, m + 1, dev).start()
            wp_move(lvl, zz, m).start()
            wq_move(lvl, zz, m, dev).wait_recv()
            if m not in (3, 6):
                wq_move(lvl, zz, m + 1, dev).start()
        wy_move(lvl).wait_send()
        for m in range(7):
            wb_move(lvl, z, m, ahead).wait_send()
            wq_move(lvl, z, m, ahead).wait_send()
            wp_move(lvl, z, m).wait()

    def back_tile(t):
        slots = [bslot[t * 4 + e] for e in range(4)]
        lhs = jnp.concatenate([at[k] for k in slots], axis=1)
        rhs = jnp.concatenate([local[k // 4] for k in slots], axis=0)
        part[t] = jnp.dot(lhs, rhs, preferred_element_type=F32)

    def c_move(lvl, n):
        return move(csend.at[n], crecv.at[lvl, n], c_s.at[n], c_r.at[lvl, n], sibling)

    def i_move(lvl, n):
        return move(isend.at[n], irecv.at[lvl, n], i_s.at[n], i_r.at[lvl, n], col_dev(n))

    def dest_chip(n):
        return chip if n == 7 else chip_at(n)

    def sum_col(lvl):
        for n in range(8):
            t = dest_chip(n) * 2 + 1 - core
            back_tile(t)
            csend[n] = encode(part[t], BWD)
            c_move(lvl, n).start()
        for n in range(8):
            t = dest_chip(n) * 2 + core
            back_tile(t)
            c_move(lvl, n).wait_recv()
            v = part[t] + decode(crecv[lvl, n], BWD)
            if n < 7:
                isend[n] = encode(v, BWD)
                i_move(lvl, n).start()
            else:
                total[...] = v
        for n in (5, 6, 4, 3, 1, 2, 0):
            i_move(lvl, n).wait_recv()
            total[...] += decode(irecv[lvl, n], BWD)
        for n in range(8):
            c_move(lvl, n).wait_send()
        for n in range(7):
            i_move(lvl, n).wait_send()

    first = jnp.where(levels[...] == 0, paths_in[...], 0.0)
    paths[0] = first
    gath[0, c] = first.astype(BF16)
    gather_col_start(0)

    eye = (
        lax.broadcasted_iota(I32, (128, 128), 0) == lax.broadcasted_iota(I32, (128, 128), 1)
    ).astype(F32).astype(BF16)
    for i in range(16):
        load(i).wait()

    @pl.loop(0, 16)
    def _(i):
        for e in range(4):
            tile = stage[i, e].astype(F32).astype(BF16)
            acat[i, :, e * 128 : (e + 1) * 128] = tile
            at[i * 4 + e] = lax.dot_general(
                eye, tile, (((1,), (1,)), ((), ())), preferred_element_type=F32
            ).astype(BF16)

    @pl.loop(0, LVLS)
    def _(lvl):
        gather_col_end(lvl)
        local[...] = gath[lvl]
        sum_row(lvl)
        level = lvl + 1
        now = jnp.where(levels[...] == level, total[...], 0.0)
        paths[level] = now

        @pl.when(lvl < LVLS - 1)
        def _():
            gath[level, c] = now.astype(BF16)
            gather_col_start(level)

    weight = jnp.where(levels[...] == 3, 1.0 + dep_in[...], 0.0) / jnp.maximum(paths[3], 1.0)
    wgt[0, r] = weight.astype(BF16)
    out[...] = jnp.zeros_like(out)

    @pl.loop(0, LVLS)
    def _(lvl):
        gather_row(lvl)
        local[...] = wgt[lvl]
        sum_col(lvl)
        level = 2 - lvl
        mask = levels[...] == level
        delta = jnp.where(mask, paths[level] * total[...], 0.0)
        out[...] += delta

        @pl.when(lvl < LVLS - 1)
        def _():
            weight = jnp.where(mask, 1.0 + delta, 0.0) / jnp.maximum(paths[level], 1.0)
            wgt[lvl + 1, r] = weight.astype(BF16)


def slots_by_source(flat, tiles, per):
    eq = (flat[None, :] == jnp.arange(tiles, dtype=I32)[:, None]).astype(I32)
    slot = jnp.arange(flat.shape[0], dtype=I32)
    before = jnp.sum(
        jnp.where((flat[:, None] == flat[None, :]) & (slot[:, None] < slot[None, :]), 1, 0), axis=0
    )
    picked = eq[:, None, :] * (before[None, None, :] == jnp.arange(per, dtype=I32)[None, :, None])
    return jnp.sum(picked * slot[None, None, :], axis=2).reshape(-1)


def shards(paths_in, dep_in, levels, tile_src, pattern):
    rows, sources = paths_in.shape
    flat = tile_src.reshape(-1)
    tiles, half = 16, rows // 2
    back = slots_by_source(flat, tiles, 4)
    pattern = pattern.reshape(64, 128, 128)
    vmem, smem = pl.BlockSpec(memory_space=pltpu.VMEM), pl.BlockSpec(memory_space=pltpu.SMEM)
    dma = pltpu.SemaphoreType.DMA
    block = (rows, sources)
    halfb = (half, sources)
    return pl.pallas_call(
        kernel,
        out_shape=jax.ShapeDtypeStruct(block, F32),
        in_specs=[smem, smem, vmem, vmem, vmem, pl.BlockSpec(memory_space=pl.ANY)],
        out_specs=vmem,
        scratch_shapes=[
            pltpu.VMEM((16, 4, 128, 128), I32),
            pltpu.VMEM((16, 128, 512), BF16),
            pltpu.VMEM((64, 128, 128), BF16),
            pltpu.VMEM((LVLS, tiles, *block), BF16),
            pltpu.VMEM((LVLS, tiles, *block), BF16),
            pltpu.VMEM((tiles, *block), BF16),
            pltpu.VMEM((tiles, *block), F32),
            pltpu.VMEM((4, *block), F32),
            pltpu.VMEM(block, F32),
            pltpu.VMEM((8, *halfb), I16),
            pltpu.VMEM((LVLS, 8, *halfb), I16),
            pltpu.VMEM((7, 2, *halfb), I16),
            pltpu.VMEM((LVLS, 7, 2, *halfb), I16),
            pltpu.VMEM((7, *halfb), I16),
            pltpu.VMEM((LVLS, 7, *halfb), I16),
            pltpu.VMEM(halfb, I16),
            pltpu.VMEM((LVLS, *halfb), I16),
            pltpu.VMEM((8, *block), I16),
            pltpu.VMEM((LVLS, 8, *block), I16),
            pltpu.VMEM((7, *block), I16),
            pltpu.VMEM((LVLS, 7, *block), I16),
            dma((16,)),
            dma((7,)), dma((LVLS, 7)), dma((8,)), dma((LVLS, 8)),
            dma((8,)), dma((LVLS, 8)), dma((7,)), dma((LVLS, 7)), dma((7,)), dma((LVLS, 7)), dma, dma((LVLS,)),
            dma, dma((LVLS,)), dma((7,)), dma((LVLS, 7)), dma((7,)), dma((LVLS, 7)), dma((7,)), dma((LVLS, 7)),
            dma((8,)), dma((LVLS, 8)), dma((7,)), dma((LVLS, 7)),
        ],
        compiler_params=pltpu.CompilerParams(
            collective_id=0, has_side_effects=True, vmem_limit_bytes=48 * 1024 * 1024
        ),
    )(flat, back, paths_in, dep_in, levels, pattern)


def solution(mesh):
    placed = (
        P(("row", "col"), None),
        P(("row", "col"), None),
        P(("row", "col"), None),
        P("row", "col", None, None),
        P("row", "col", None, None, None, None),
    )
    return jax.shard_map(
        shards, mesh=mesh, in_specs=placed, out_specs=P(("row", "col"), None), check_vma=False
    )
```

```python
import jax
import jax.numpy as jnp
from jax import lax
from jax.experimental import pallas as pl
from jax.experimental.pallas import tpu as pltpu
from jax.sharding import PartitionSpec as P

MESH = pl.DeviceIdType.MESH
F32, BF16, I16, I32 = jnp.float32, jnp.bfloat16, jnp.int16, jnp.int32

ZS, XS, HI = 8, 4, 2
TILE, BAND, TILES = 128, 4, 16
LVLS = 3
NB = 1
PR = 80
QR = TILE - PR
FWD = (-5.0, 1365.0)
BWD = (-44.0, 744.0)
LN2 = 0.6931471805599453


def encode(x, code):
    low, steps = code
    v = jnp.log(jnp.maximum(x, 2.0**low)) * (steps / LN2) + (0.5 - low * steps)
    return (v.astype(I32) - 32768).astype(I16)


def decode(c, code):
    low, steps = code
    v = c.astype(I32).astype(F32)
    x = jnp.exp(v * (LN2 / steps) + (32768.0 / steps + low) * LN2)
    return jnp.where(v > -32768.0, x, 0.0)


def kernel(
    tsrc, bslot, paths_hbm, dep_hbm, levels_hbm, pattern, out,
    paths_in, dep_in, levels,
    stage, acat, at, gath, wgt, local, part, paths, total,
    ysend, yrecv, zsend, zrecv, qsend, qrecv, fsend, frecv, csend, crecv, isend, irecv,
    load_sem, in_sem,
    ag_s, ag_r, sib_s, sib_r, y_s, y_r, z_s, z_r, q_s, q_r, f_s, f_r,
    wz_s, wz_r, wy_s, wy_r, wq_s, wq_r, wf_s, wf_r, c_s, c_r, i_s, i_r,
):
    r, c = lax.axis_index("row"), lax.axis_index("col")
    z, y = r // 2, r % 2
    chip, core = c // 2, c % 2
    yhi, x = chip // XS, chip % XS
    lanes = gath.shape[-1]

    def load(i):
        return pltpu.make_async_copy(pattern.at[pl.ds(i * BAND, BAND)], stage.at[i], load_sem.at[i])

    inputs = [
        pltpu.make_async_copy(src, dst, in_sem.at[n])
        for n, (src, dst) in enumerate(
            [(paths_hbm, paths_in), (levels_hbm, levels), (dep_hbm, dep_in)]
        )
    ]
    for copy in inputs:
        copy.start()
    for i in range(TILES):
        load(i).start()

    def z_off(j):
        return (1 - 2 * core) * jnp.where(j % 2 == 1, (7 - j) // 2, -((8 - j) // 2))

    def z_to(j):
        return (z + z_off(j) + ZS) % ZS

    def c_to(n, sign=1):
        dx, dy = (7 - n) % XS, (7 - n) // XS
        return ((yhi + dy) % HI) * XS + (x + sign * dx + XS) % XS

    def z_dev(hops):
        return {"row": z_hop(hops) * 2 + y, "col": c}

    def z_hop(hops):
        return (z + (1 - 2 * core) * hops + ZS) % ZS

    def c_dev(n):
        return {"row": r, "col": c_to(n) * 2 + core}

    across = {"row": z * 2 + 1 - y, "col": c}
    sibling = {"row": r, "col": chip * 2 + 1 - core}

    def move(src, dst, ssem, rsem, dev):
        return pltpu.make_async_remote_copy(
            src_ref=src, dst_ref=dst, send_sem=ssem, recv_sem=rsem, device_id=dev, device_id_type=MESH
        )

    barrier = pltpu.get_barrier_semaphore()
    partners = [across, sibling] + [z_dev(hops) for hops in (2, 1, -1, -2)] + [c_dev(n) for n in range(7)]
    for dev in partners:
        pl.semaphore_signal(barrier, inc=1, device_id=dev, device_id_type=MESH)
    pl.semaphore_wait(barrier, len(partners))

    def ag_move(b, lvl, n, place):
        ref = gath.at[b, lvl, place]
        return move(ref, ref, ag_s.at[b, n], ag_r.at[b, lvl, n], c_dev(n))

    def sib_move(b, lvl, n, place):
        ref = gath.at[b, lvl, place]
        return move(ref, ref, sib_s.at[b, n], sib_r.at[b, lvl, n], sibling)

    def y_move(b, lvl, j):
        return move(ysend.at[b, j], yrecv.at[b, lvl, j], y_s.at[b, j], y_r.at[b, lvl, j], across)

    def hop_dev(j):
        return z_dev((2, 1, -1, 2, -2, 1, -1)[j])

    def z_move(b, lvl, j):
        return move(zsend.at[b, j], zrecv.at[b, lvl, j], z_s.at[b, j], z_r.at[b, lvl, j], hop_dev(j))

    def q_move(b, lvl, j):
        return move(qsend.at[b, j], qrecv.at[b, lvl, j], q_s.at[b, j], q_r.at[b, lvl, j], hop_dev(j))

    def f_move(b, lvl):
        return move(fsend.at[b, 0], frecv.at[b, lvl, 0], f_s.at[b, 0], f_r.at[b, lvl, 0], across)

    def z_go(b, lvl, j):
        y_move(b, lvl, j).wait_recv()
        v = part[b, 0, j, :PR] + decode(yrecv[b, lvl, j], FWD)
        for m in {3: (1, 0), 4: (2,)}.get(j, ()):
            z_move(b, lvl, m).wait_recv()
            v += decode(zrecv[b, lvl, m], FWD)
        zsend[b, j] = encode(v, FWD)
        z_move(b, lvl, j).start()

    def q_go(b, lvl, j):
        joined = {3: (1, 0), 4: (2,)}.get(j, ())
        for m in joined:
            q_move(b, lvl, m).wait_recv()
        for k in range(2):
            v = part[b, k, j, PR:]
            for m in joined:
                v += decode(qrecv[b, lvl, m, k], FWD)
            qsend[b, j, k] = encode(v, FWD)
        q_move(b, lvl, j).start()

    def fwd_send(b, lvl, value):
        gath[b, lvl, c] = value.astype(BF16)
        for n in range(7):
            ag_move(b, lvl, n, c).start()
        sib_move(b, lvl, 7, c).start()

    def fwd_pass(b, lvl):
        for n in (6, 4, 5, 3, 2, 0, 1):
            place = c_to(n, -1) * 2 + core
            ag_move(b, lvl, n, place).wait_recv()
            sib_move(b, lvl, n, place).start()

    def fwd_tile(b, i):
        rhs = jnp.concatenate([local[b, tsrc[e, i]] for e in range(BAND)], axis=0)
        return jnp.dot(acat[i], rhs, preferred_element_type=F32)

    def fwd_work(b, lvl):
        for n in range(8):
            sib_move(b, lvl, n, c).wait_recv()
        local[b] = gath[b, lvl]

        def pair(j):
            for k, i in ((1, z_to(j) * 2 + 1 - y), (0, z_to(j) * 2 + y)):
                part[b, k, j] = fwd_tile(b, i)
            ysend[b, j] = encode(part[b, 1, j, :PR], FWD)
            y_move(b, lvl, j).start()

        for j in range(3):
            pair(j)
            q_go(b, lvl, j)

        for j in (5, 6, 3, 4, 7):
            pair(j)
            if j == 6:
                q_go(b, lvl, 5)
                q_go(b, lvl, 6)

    def fwd_mid(b, lvl):
        for j in (0, 1, 2):
            z_go(b, lvl, j)
        for j in (3, 4):
            q_go(b, lvl, j)
        for j in (5, 6, 3, 4):
            z_go(b, lvl, j)

    def fwd_end(b, lvl):
        own = part[b, 0, 7, PR:]
        other = part[b, 1, 7, PR:]
        for j in (6, 5, 4, 3):
            q_move(b, lvl, j).wait_recv()
            own += decode(qrecv[b, lvl, j, 0], FWD)
            other += decode(qrecv[b, lvl, j, 1], FWD)
        fsend[b, 0] = encode(other, FWD)
        f_move(b, lvl).start()
        y_move(b, lvl, 7).wait_recv()
        mine = part[b, 0, 7, :PR] + decode(yrecv[b, lvl, 7], FWD)
        for j in (6, 5, 4, 3):
            z_move(b, lvl, j).wait_recv()
            mine += decode(zrecv[b, lvl, j], FWD)
        total[b, :PR] = mine
        f_move(b, lvl).wait()
        total[b, PR:] = own + decode(frecv[b, lvl, 0], FWD)
        for j in range(7):
            q_move(b, lvl, j).wait_send()
        for n in range(7):
            ag_move(b, lvl, n, c).wait_send()
            z_move(b, lvl, n).wait_send()
        for n in range(8):
            sib_move(b, lvl, n, c).wait_send()
            y_move(b, lvl, n).wait_send()
        level = lvl + 1
        value = jnp.where(levels_of(b) == level, total[b], 0.0)
        paths[b, level] = value
        return value

    def relay_dev(j):
        return z_dev((2, -2, 1, -1, 2, 1, -1)[j])

    def origin(j):
        return z_hop((-2, 2, -1, 1, -4, -3, 3)[j])

    def wz_move(b, lvl, j, zz):
        ref = wgt.at[b, lvl, zz * 2 + y]
        return move(ref, ref, wz_s.at[b, j], wz_r.at[b, lvl, j], relay_dev(j))

    def wq_move(b, lvl, j, zz):
        ref = wgt.at[b, lvl, zz * 2 + 1 - y, pl.ds(PR, QR)]
        return move(ref, ref, wq_s.at[b, j], wq_r.at[b, lvl, j], relay_dev(j))

    def wy_move(b, lvl, j, zz):
        ref = wgt.at[b, lvl, zz * 2 + y, pl.ds(0, PR)]
        return move(ref, ref, wy_s.at[b, j], wy_r.at[b, lvl, j], across)

    def wf_move(b, lvl):
        ref = wgt.at[b, lvl, r, pl.ds(PR, QR)]
        return move(ref, ref, wf_s.at[b, 0], wf_r.at[b, lvl, 0], across)

    def c_move(b, lvl, n):
        return move(csend.at[b, n], crecv.at[b, lvl, n], c_s.at[b, n], c_r.at[b, lvl, n], sibling)

    def i_move(b, lvl, n):
        return move(isend.at[b, n], irecv.at[b, lvl, n], i_s.at[b, n], i_r.at[b, lvl, n], c_dev(n))

    def bwd_send(b, lvl, value):
        wgt[b, lvl, r] = value.astype(BF16)
        wf_move(b, lvl).start()
        for j in range(4):
            wz_move(b, lvl, j, z).start()
        wy_move(b, lvl, 7, z).start()

    def bwd_pass(b, lvl):
        wf_move(b, lvl).wait_recv()
        for j in range(4):
            wq_move(b, lvl, j, z).start()
        def take(go, j):
            go(b, lvl, j, origin(j)).wait_recv()
            for m in {0: (4, 5), 1: (6,)}.get(j, ()):
                go(b, lvl, m, origin(j)).start()
            if go is wz_move:
                wy_move(b, lvl, j, origin(j)).start()

        for j in (2, 3, 0, 1):
            take(wz_move, j)
        take(wq_move, 0)
        take(wq_move, 1)
        for j in (5, 6, 4):
            take(wz_move, j)
        for j in (2, 3, 5, 6, 4):
            take(wq_move, j)

    def bwd_tile(b, t):
        slots = [bslot[t * BAND + e] for e in range(BAND)]
        lhs = jnp.concatenate([at[k] for k in slots], axis=1)
        rhs = jnp.concatenate([local[b, k % TILES] for k in slots], axis=0)
        return jnp.dot(lhs, rhs, preferred_element_type=F32)

    def bwd_work(b, lvl):
        for j in range(8):
            wy_move(b, lvl, j, z).wait_recv()
        local[b] = wgt[b, lvl]

        @pl.loop(0, 8)
        def _(n):
            csend[b, n] = encode(bwd_tile(b, c_to(n) * 2 + 1 - core), BWD)
            c_move(b, lvl, n).start()

        @pl.loop(0, 8)
        def _(n):
            part[b, 0, n] = bwd_tile(b, c_to(n) * 2 + core)

    def bwd_mid(b, lvl):
        for n in range(7):
            c_move(b, lvl, n).wait_recv()
            v = part[b, 0, n] + decode(crecv[b, lvl, n], BWD)
            isend[b, n] = encode(v, BWD)
            i_move(b, lvl, n).start()

        c_move(b, lvl, 7).wait_recv()
        total[b] = part[b, 0, 7] + decode(crecv[b, lvl, 7], BWD)

    def bwd_end(b, lvl):
        for n in (6, 4, 5, 3, 2, 0, 1):
            i_move(b, lvl, n).wait_recv()
            total[b] += decode(irecv[b, lvl, n], BWD)
        for n in range(7):
            wz_move(b, lvl, n, z).wait_send()
            wq_move(b, lvl, n, z).wait_send()
            i_move(b, lvl, n).wait_send()
        for n in range(8):
            wy_move(b, lvl, n, z).wait_send()
            c_move(b, lvl, n).wait_send()
        wf_move(b, lvl).wait_send()
        level = 2 - lvl
        mask = levels_of(b) == level
        delta = jnp.where(mask, paths[b, level] * total[b], 0.0)
        out[:, b * lanes : (b + 1) * lanes] += delta
        return jnp.where(mask, 1.0 + delta, 0.0) / jnp.maximum(paths[b, level], 1.0)

    def levels_of(b):
        return levels[:, b * lanes : (b + 1) * lanes]

    def fwd_next(b, lvl):
        value = fwd_end(b, lvl)

        @pl.when(lvl < LVLS - 1)
        def _():
            fwd_send(b, lvl + 1, value)

        @pl.when(lvl == LVLS - 1)
        def _():
            turn(b, value)

    def turn(b, value):
        top = jnp.where(levels_of(b) == 3, 1.0 + dep_in[:, b * lanes : (b + 1) * lanes], 0.0)
        bwd_send(b, 0, top / jnp.maximum(value, 1.0))

    def bwd_next(b, lvl):
        value = bwd_end(b, lvl)

        @pl.when(lvl < LVLS - 1)
        def _():
            bwd_send(b, lvl + 1, value)

    inputs[0].wait()
    inputs[1].wait()
    for b in range(NB):
        value = jnp.where(levels_of(b) == 0, paths_in[:, b * lanes : (b + 1) * lanes], 0.0)
        paths[b, 0] = value
        fwd_send(b, 0, value)
    inputs[2].wait()
    out[...] = jnp.zeros_like(out)

    eye = (
        lax.broadcasted_iota(I32, (TILE, TILE), 0) == lax.broadcasted_iota(I32, (TILE, TILE), 1)
    ).astype(F32).astype(BF16)
    for i in range(TILES):
        load(i).wait()

    @pl.loop(0, TILES)
    def _(i):
        for e in range(BAND):
            tile = stage[i, e].astype(F32).astype(BF16)
            acat[i, :, e * TILE : (e + 1) * TILE] = tile
            at[e * TILES + i] = lax.dot_general(
                eye, tile, (((1,), (1,)), ((), ())), preferred_element_type=F32
            ).astype(BF16)

    batches = range(NB)

    def each(*stages):
        def body(lvl):
            for stage in stages:
                for b in batches:
                    stage(b, lvl)

        return body

    pl.loop(0, LVLS)(each(fwd_pass, fwd_work, fwd_mid, fwd_next))
    pl.loop(0, LVLS)(each(bwd_pass, bwd_work, bwd_mid, bwd_next))


def slots_by_source(flat):
    slots = jnp.arange(TILES * BAND, dtype=I32)
    same = (flat[:, None] == flat[None, :]) & (slots[:, None] < slots[None, :])
    before = jnp.sum(same.astype(I32), axis=0)
    mine = flat[None, :] == jnp.arange(TILES, dtype=I32)[:, None]
    nth = before[None, :] == jnp.arange(BAND, dtype=I32)[:, None]
    picked = mine[:, None, :] & nth[None, :, :]
    return jnp.sum(jnp.where(picked, slots, 0), axis=2).reshape(-1)


def shards(paths_in, dep_in, levels, tile_src, pattern):
    rows, sources = paths_in.shape
    by_slot = tile_src[0, 0].T
    back = slots_by_source(by_slot.reshape(-1))
    pattern = pattern.reshape(TILES * BAND, TILE, TILE)
    vmem, smem, hbm = (
        pl.BlockSpec(memory_space=m) for m in (pltpu.VMEM, pltpu.SMEM, pltpu.HBM)
    )
    block = (rows, sources // NB)
    whole = (rows, sources)

    def dma(*shape):
        return pltpu.SemaphoreType.DMA(shape)

    def pairs(*counts):
        return [d for n in counts for d in (dma(NB, n), dma(NB, LVLS, n))]

    def slots(*dims):
        shape = (*dims, sources // NB)
        return [pltpu.VMEM((NB, *shape), I16), pltpu.VMEM((NB, LVLS, *shape), I16)]

    return pl.pallas_call(
        kernel,
        out_shape=jax.ShapeDtypeStruct(whole, F32),
        in_specs=[smem, smem, hbm, hbm, hbm, hbm],
        out_specs=vmem,
        scratch_shapes=[
            pltpu.VMEM(whole, F32),
            pltpu.VMEM(whole, F32),
            pltpu.VMEM(whole, I32),
            pltpu.VMEM((TILES, BAND, TILE, TILE), I32),
            pltpu.VMEM((TILES, TILE, BAND * TILE), BF16),
            pltpu.VMEM((TILES * BAND, TILE, TILE), BF16),
            pltpu.VMEM((NB, LVLS, TILES, *block), BF16),
            pltpu.VMEM((NB, LVLS, TILES, *block), BF16),
            pltpu.VMEM((NB, TILES, *block), BF16),
            pltpu.VMEM((NB, 2, 8, *block), F32),
            pltpu.VMEM((NB, 4, *block), F32),
            pltpu.VMEM((NB, *block), F32),
            *slots(8, PR), *slots(7, PR), *slots(7, 2, QR), *slots(1, QR), *slots(8, rows), *slots(7, rows),
            dma(TILES),
            dma(3),
            *pairs(7, 8, 8, 7, 7, 1),
            *pairs(7, 8, 7, 1, 8, 7),
        ],
        compiler_params=pltpu.CompilerParams(
            collective_id=0, has_side_effects=True, vmem_limit_bytes=56 * 1024 * 1024
        ),
    )(by_slot, back, paths_in, dep_in, levels, pattern)


def solution(mesh):
    placed = (
        P(("row", "col"), None),
        P(("row", "col"), None),
        P(("row", "col"), None),
        P("row", "col", None, None),
        P("row", "col", None, None, None, None),
    )
    return jax.shard_map(
        shards, mesh=mesh, in_specs=placed, out_specs=P(("row", "col"), None), check_vma=False
    )
```

```python
import jax
import jax.numpy as jnp
from jax import lax
from jax.experimental import pallas as pl
from jax.experimental.pallas import tpu as pltpu
from jax.sharding import PartitionSpec as P

MESH = pl.DeviceIdType.MESH
F32, BF16, I16, I32 = jnp.float32, jnp.bfloat16, jnp.int16, jnp.int32

ZS, XS, HI = 8, 4, 2
TILE, BAND, TILES = 128, 4, 16
LVLS = 3
NB = 1
PR = 80
QR = TILE - PR
ORDER = (0, 1, 2, 5, 6, 3, 4, 7)
FWD = (-5.0, 1365.0)
BWD = (-44.0, 744.0)
LN2 = 0.6931471805599453


def encode(x, code):
    low, steps = code
    v = jnp.log(jnp.maximum(x, 2.0**low)) * (steps / LN2) + (0.5 - low * steps)
    return (v.astype(I32) - 32768).astype(I16)


def decode(c, code):
    low, steps = code
    v = c.astype(I32).astype(F32)
    x = jnp.exp(v * (LN2 / steps) + (32768.0 / steps + low) * LN2)
    return jnp.where(v > -32768.0, x, 0.0)


def kernel(
    tsrc, bslot, paths_hbm, dep_hbm, levels_hbm, pattern, out,
    paths_in, dep_in, levels,
    stage, acat, at, gath, wgtp, wgtq, local, part, paths, total,
    ysend, yrecv, zsend, zrecv, qsend, qrecv, fsend, frecv, csend, crecv, isend, irecv,
    load_sem, in_sem,
    ag_s, ag_r, sib_s, sib_r, y_s, y_r, z_s, z_r, q_s, q_r, f_s, f_r,
    wz_s, wz_r, wy_s, wy_r, wq_s, wq_r, wf_s, wf_r, c_s, c_r, i_s, i_r,
):
    r, c = lax.axis_index("row"), lax.axis_index("col")
    z, y = r // 2, r % 2
    chip, core = c // 2, c % 2
    yhi, x = chip // XS, chip % XS
    lanes = gath.shape[-1]

    def load(i):
        return pltpu.make_async_copy(pattern.at[pl.ds(i * BAND, BAND)], stage.at[i], load_sem.at[i])

    inputs = [
        pltpu.make_async_copy(src, dst, in_sem.at[n])
        for n, (src, dst) in enumerate(
            [(paths_hbm, paths_in), (levels_hbm, levels), (dep_hbm, dep_in)]
        )
    ]
    for copy in inputs:
        copy.start()
    for i in range(TILES):
        load(i).start()

    def z_off(j):
        return (1 - 2 * core) * jnp.where(j % 2 == 1, (7 - j) // 2, -((8 - j) // 2))

    def z_to(j):
        return (z + z_off(j) + ZS) % ZS

    def c_to(n, sign=1):
        dx, dy = (7 - n) % XS, (7 - n) // XS
        return ((yhi + dy) % HI) * XS + (x + sign * dx + XS) % XS

    def z_dev(hops):
        return {"row": z_hop(hops) * 2 + y, "col": c}

    def z_hop(hops):
        return (z + (1 - 2 * core) * hops + ZS) % ZS

    def c_dev(n):
        return {"row": r, "col": c_to(n) * 2 + core}

    across = {"row": z * 2 + 1 - y, "col": c}
    sibling = {"row": r, "col": chip * 2 + 1 - core}

    def move(src, dst, ssem, rsem, dev):
        return pltpu.make_async_remote_copy(
            src_ref=src, dst_ref=dst, send_sem=ssem, recv_sem=rsem, device_id=dev, device_id_type=MESH
        )

    barrier = pltpu.get_barrier_semaphore()
    partners = [across, sibling] + [z_dev(hops) for hops in (2, 1, -1, -2)] + [c_dev(n) for n in range(7)]
    for dev in partners:
        pl.semaphore_signal(barrier, inc=1, device_id=dev, device_id_type=MESH)
    pl.semaphore_wait(barrier, len(partners))

    def ag_move(b, lvl, n, place):
        ref = gath.at[b, lvl, place]
        return move(ref, ref, ag_s.at[b, n], ag_r.at[b, lvl, n], c_dev(n))

    def sib_move(b, lvl, n):
        ref = gath.at[b, lvl, core * 8 + c_to(n, -1)]
        return move(ref, ref, sib_s.at[b, n], sib_r.at[b, lvl, n], sibling)

    def y_move(b, lvl, j):
        return move(ysend.at[b, j], yrecv.at[b, lvl, j], y_s.at[b, j], y_r.at[b, lvl, j], across)

    def hop_dev(j):
        return z_dev((2, 1, -1, 2, -2, 1, -1)[j])

    def z_move(b, lvl, j):
        return move(zsend.at[b, j], zrecv.at[b, lvl, j], z_s.at[b, j], z_r.at[b, lvl, j], hop_dev(j))

    def q_move(b, lvl, j):
        return move(qsend.at[b, j], qrecv.at[b, lvl, j], q_s.at[b, j], q_r.at[b, lvl, j], hop_dev(j))

    def f_move(b, lvl):
        return move(fsend.at[b, 0], frecv.at[b, lvl, 0], f_s.at[b, 0], f_r.at[b, lvl, 0], across)

    def y_sum(b, lvl, j):
        y_move(b, lvl, j).wait_recv()
        return part[b, 0, j, :PR] + decode(yrecv[b, lvl, j], FWD)

    def z_go(b, lvl, j):
        v = y_sum(b, lvl, j)
        for m in {3: (1, 0), 4: (2,)}.get(j, ()):
            z_move(b, lvl, m).wait_recv()
            v += decode(zrecv[b, lvl, m], FWD)
        zsend[b, j] = encode(v, FWD)
        z_move(b, lvl, j).start()

    def q_go(b, lvl, j):
        joined = {3: (1, 0), 4: (2,)}.get(j, ())
        for m in joined:
            q_move(b, lvl, m).wait_recv()
        for k in range(2):
            v = part[b, k, j, PR:]
            for m in joined:
                v += decode(qrecv[b, lvl, m, k], FWD)
            qsend[b, j, k] = encode(v, FWD)
        q_move(b, lvl, j).start()

    def fwd_send(b, lvl, value):
        gath[b, lvl, core * 8 + chip] = value.astype(BF16)
        for n in range(7):
            ag_move(b, lvl, n, core * 8 + chip).start()
        sib_move(b, lvl, 7).start()

    def fwd_pass(b, lvl):
        local[b, core * 8 + chip] = gath[b, lvl, core * 8 + chip]
        for n in (6, 4, 5, 3, 2, 0, 1):
            place = core * 8 + c_to(n, -1)
            ag_move(b, lvl, n, place).wait_recv()
            sib_move(b, lvl, n).start()
            local[b, place] = gath[b, lvl, place]

    def fwd_tile(b, i):
        rhs = jnp.concatenate([local[b, tsrc[e, i]] for e in range(BAND)], axis=0)
        return jnp.dot(acat[i], rhs, preferred_element_type=F32)

    def fwd_work(b, lvl):
        for n in (7, 6, 4, 5, 3, 2, 0, 1):
            sib_move(b, lvl, n).wait_recv()
            local[b, (1 - core) * 8 + c_to(n, -1)] = gath[b, lvl, (1 - core) * 8 + c_to(n, -1)]

        def pair(j):
            for k, i in ((1, z_to(j) * 2 + 1 - y), (0, z_to(j) * 2 + y)):
                part[b, k, j] = fwd_tile(b, i)
            ysend[b, j] = encode(part[b, 1, j, :PR], FWD)
            y_move(b, lvl, j).start()

        for j in ORDER:
            pair(j)
            if j < 3:
                q_go(b, lvl, j)
            if j == 6:
                q_go(b, lvl, 5)
                q_go(b, lvl, 6)

        for n in range(7):
            ag_move(b, lvl, n, chip).wait_send()
        for k in range(8):
            sib_move(b, lvl, k).wait_send()

    def fwd_mid(b, lvl):
        for j in (0, 1, 2):
            z_go(b, lvl, j)
        for j in (3, 4):
            q_go(b, lvl, j)
        for j in (5, 6, 3, 4):
            z_go(b, lvl, j)

    def fwd_end(b, lvl, go):
        mine = y_sum(b, lvl, 7)
        own = part[b, 0, 7, PR:]
        other = part[b, 1, 7, PR:]
        for j in (6, 5, 4, 3):
            q_move(b, lvl, j).wait_recv()
            own += decode(qrecv[b, lvl, j, 0], FWD)
            other += decode(qrecv[b, lvl, j, 1], FWD)
        fsend[b, 0] = encode(other, FWD)
        f_move(b, lvl).start()
        total[b, PR:] = own
        for j in (6, 5, 4, 3):
            z_move(b, lvl, j).wait_recv()
            mine += decode(zrecv[b, lvl, j], FWD)
        total[b, :PR] = mine
        f_move(b, lvl).wait()
        total[b, PR:] += decode(frecv[b, lvl, 0], FWD)
        level = lvl + 1
        value = jnp.where(levels_of(b) == level, total[b], 0.0)
        paths[b, level] = value
        go(value)
        for j in range(7):
            q_move(b, lvl, j).wait_send()
            z_move(b, lvl, j).wait_send()
        for j in range(8):
            y_move(b, lvl, j).wait_send()

    def relay_dev(j):
        return z_dev((2, -2, 1, -1, 2, 1, -1)[j])

    def origin(j):
        return z_hop((-2, 2, -1, 1, -4, -3, 3)[j])

    def slot_from(j):
        return {4: 1, 5: 1, 6: 2}.get(j, 0)

    def wz_move(b, lvl, j):
        src, dst = wgtp.at[b, lvl, 0, slot_from(j)], wgtp.at[b, lvl, 0, 1 + j]
        return move(src, dst, wz_s.at[b, j], wz_r.at[b, lvl, j], relay_dev(j))

    def wq_move(b, lvl, j):
        src, dst = wgtq.at[b, lvl, slot_from(j)], wgtq.at[b, lvl, 1 + j]
        return move(src, dst, wq_s.at[b, j], wq_r.at[b, lvl, j], relay_dev(j))

    def wy_move(b, lvl, g):
        src, dst = wgtp.at[b, lvl, 0, g], wgtp.at[b, lvl, 1, g]
        return move(src, dst, wy_s.at[b, g], wy_r.at[b, lvl, g], across)

    def wf_move(b, lvl):
        ref = wgtq.at[b, lvl, 0, y]
        return move(ref, ref, wf_s.at[b, 0], wf_r.at[b, lvl, 0], across)

    def c_move(b, lvl, n):
        return move(csend.at[b, n], crecv.at[b, lvl, n], c_s.at[b, n], c_r.at[b, lvl, n], sibling)

    def i_move(b, lvl, n):
        return move(isend.at[b, n], irecv.at[b, lvl, n], i_s.at[b, n], i_r.at[b, lvl, n], c_dev(n))

    def bwd_send(b, lvl, value):
        value = value.astype(BF16)
        wgtq[b, lvl, 0, y] = value[PR:]
        wf_move(b, lvl).start()
        wgtp[b, lvl, 0, 0] = value[:PR]
        for j in range(4):
            wz_move(b, lvl, j).start()
        wy_move(b, lvl, 0).start()

    def keep_p(b, lvl, side, slot):
        zz = origin(slot - 1) if slot else z
        local[b, zz * 2 + (1 - y if side else y), :PR] = wgtp[b, lvl, side, slot]

    def keep_q(b, lvl, slot):
        zz = origin(slot - 1) if slot else z
        local[b, pl.ds(zz * 2, 2), PR:] = wgtq[b, lvl, slot]

    def bwd_pass(b, lvl):
        wf_move(b, lvl).wait_recv()
        for j in range(4):
            wq_move(b, lvl, j).start()
        for j in (2, 3, 0, 1):
            wz_move(b, lvl, j).wait_recv()
            for m in {0: (4, 5), 1: (6,)}.get(j, ()):
                wz_move(b, lvl, m).start()
            wy_move(b, lvl, 1 + j).start()
        for j in (0, 1):
            wq_move(b, lvl, j).wait_recv()
            for m in {0: (4, 5), 1: (6,)}[j]:
                wq_move(b, lvl, m).start()
        for slot in range(5):
            keep_p(b, lvl, 0, slot)
        for slot in range(3):
            keep_q(b, lvl, slot)
        for j in (5, 6, 4):
            wz_move(b, lvl, j).wait_recv()
            wy_move(b, lvl, 1 + j).start()
        for slot in range(5, 8):
            keep_p(b, lvl, 0, slot)
        for j in (2, 3, 5, 6, 4):
            wq_move(b, lvl, j).wait_recv()
            keep_q(b, lvl, 1 + j)

    def bwd_tile(b, t):
        slots = [bslot[t * BAND + e] for e in range(BAND)]
        lhs = jnp.concatenate([at[k] for k in slots], axis=1)
        rhs = jnp.concatenate([local[b, k % TILES] for k in slots], axis=0)
        return jnp.dot(lhs, rhs, preferred_element_type=F32)

    def bwd_work(b, lvl):
        for slot in (0, 3, 4, 1, 2, 6, 7, 5):
            wy_move(b, lvl, slot).wait_recv()
            keep_p(b, lvl, 1, slot)

        def sums(n):
            part[b, 0, n] = bwd_tile(b, c_to(n) * 2 + core)
            c_move(b, lvl, n).wait_recv()
            v = part[b, 0, n] + decode(crecv[b, lvl, n], BWD)
            if n == 7:
                total[b] = v
                return
            isend[b, n] = encode(v, BWD)
            i_move(b, lvl, n).start()

        ahead = 3
        for n in range(8 + ahead):
            if n < 8:
                csend[b, n] = encode(bwd_tile(b, c_to(n) * 2 + 1 - core), BWD)
                c_move(b, lvl, n).start()
            if n >= ahead:
                sums(n - ahead)
        for j in range(7):
            wz_move(b, lvl, j).wait_send()
            wq_move(b, lvl, j).wait_send()
        for g in range(8):
            wy_move(b, lvl, g).wait_send()
        wf_move(b, lvl).wait_send()

    def bwd_end(b, lvl, go):
        level = 2 - lvl
        for n in (6, 4, 5, 3, 2, 0, 1):
            i_move(b, lvl, n).wait_recv()
            total[b] += decode(irecv[b, lvl, n], BWD)
        mask = levels_of(b) == level
        counts = paths[b, level]
        delta = jnp.where(mask, counts * total[b], 0.0)
        go(jnp.where(mask, 1.0 + delta, 0.0) / jnp.maximum(counts, 1.0))
        out[:, b * lanes : (b + 1) * lanes] += delta
        for n in range(7):
            i_move(b, lvl, n).wait_send()
        for n in range(8):
            c_move(b, lvl, n).wait_send()

    def levels_of(b):
        return levels[:, b * lanes : (b + 1) * lanes]

    def fwd_next(b, lvl):
        def go(value):
            @pl.when(lvl < LVLS - 1)
            def _():
                fwd_send(b, lvl + 1, value)

            @pl.when(lvl == LVLS - 1)
            def _():
                top = 1.0 + dep_in[:, b * lanes : (b + 1) * lanes]
                bwd_send(b, 0, jnp.where(levels_of(b) == 3, top, 0.0) / jnp.maximum(value, 1.0))

        fwd_end(b, lvl, go)

    def bwd_next(b, lvl):
        def go(value):
            @pl.when(lvl < LVLS - 1)
            def _():
                bwd_send(b, lvl + 1, value)

        bwd_end(b, lvl, go)

    inputs[0].wait()
    inputs[1].wait()
    for b in range(NB):
        value = jnp.where(levels_of(b) == 0, paths_in[:, b * lanes : (b + 1) * lanes], 0.0)
        paths[b, 0] = value
        fwd_send(b, 0, value)
    inputs[2].wait()
    out[...] = jnp.zeros_like(out)

    eye = (
        lax.broadcasted_iota(I32, (TILE, TILE), 0) == lax.broadcasted_iota(I32, (TILE, TILE), 1)
    ).astype(F32).astype(BF16)
    for i in range(TILES):
        load(i).wait()

    @pl.loop(0, TILES)
    def _(i):
        for e in range(BAND):
            tile = stage[i, e].astype(F32).astype(BF16)
            acat[i, :, e * TILE : (e + 1) * TILE] = tile
            at[e * TILES + i] = lax.dot_general(
                eye, tile, (((1,), (1,)), ((), ())), preferred_element_type=F32
            ).astype(BF16)

    batches = range(NB)

    def each(*stages):
        def body(lvl):
            for stage in stages:
                for b in batches:
                    stage(b, lvl)

        return body

    pl.loop(0, LVLS)(each(fwd_pass, fwd_work, fwd_mid, fwd_next))
    pl.loop(0, LVLS)(each(bwd_pass, bwd_work, bwd_next))


def slots_by_source(flat):
    slots = jnp.arange(TILES * BAND, dtype=I32)
    same = (flat[:, None] == flat[None, :]) & (slots[:, None] < slots[None, :])
    before = jnp.sum(same.astype(I32), axis=0)
    mine = flat[None, :] == jnp.arange(TILES, dtype=I32)[:, None]
    nth = before[None, :] == jnp.arange(BAND, dtype=I32)[:, None]
    picked = mine[:, None, :] & nth[None, :, :]
    return jnp.sum(jnp.where(picked, slots, 0), axis=2).reshape(-1)


def shards(paths_in, dep_in, levels, tile_src, pattern):
    rows, sources = paths_in.shape
    by_slot = tile_src[0, 0].T
    back = slots_by_source(by_slot.reshape(-1))
    by_slot = by_slot % 2 * 8 + by_slot // 2
    pattern = pattern.reshape(TILES * BAND, TILE, TILE)
    vmem, smem, hbm = (
        pl.BlockSpec(memory_space=m) for m in (pltpu.VMEM, pltpu.SMEM, pltpu.HBM)
    )
    block = (rows, sources // NB)
    whole = (rows, sources)

    def dma(*shape):
        return pltpu.SemaphoreType.DMA(shape)

    def pairs(*counts):
        return [d for n in counts for d in (dma(NB, n), dma(NB, LVLS, n))]

    def slots(*dims):
        shape = (*dims, sources // NB)
        return [pltpu.VMEM((NB, *shape), I16), pltpu.VMEM((NB, LVLS, *shape), I16)]

    return pl.pallas_call(
        kernel,
        out_shape=jax.ShapeDtypeStruct(whole, F32),
        in_specs=[smem, smem, hbm, hbm, hbm, hbm],
        out_specs=vmem,
        scratch_shapes=[
            pltpu.VMEM(whole, F32),
            pltpu.VMEM(whole, F32),
            pltpu.VMEM(whole, I32),
            pltpu.VMEM((TILES, BAND, TILE, TILE), I32),
            pltpu.VMEM((TILES, TILE, BAND * TILE), BF16),
            pltpu.VMEM((TILES * BAND, TILE, TILE), BF16),
            pltpu.VMEM((NB, LVLS, TILES, *block), BF16),
            pltpu.VMEM((NB, LVLS, 2, 8, PR, block[1]), BF16),
            pltpu.VMEM((NB, LVLS, 8, 2, QR, block[1]), BF16),
            pltpu.VMEM((NB, TILES, *block), BF16),
            pltpu.VMEM((NB, 2, 8, *block), F32),
            pltpu.VMEM((NB, 4, *block), F32),
            pltpu.VMEM((NB, *block), F32),
            *slots(8, PR), *slots(7, PR), *slots(7, 2, QR), *slots(1, QR), *slots(8, rows), *slots(7, rows),
            dma(TILES),
            dma(3),
            *pairs(7, 8, 8, 7, 7, 1),
            *pairs(7, 8, 7, 1, 8, 7),
        ],
        compiler_params=pltpu.CompilerParams(
            collective_id=0, has_side_effects=True, vmem_limit_bytes=56 * 1024 * 1024
        ),
    )(by_slot, back, paths_in, dep_in, levels, pattern)


def solution(mesh):
    placed = (
        P(("row", "col"), None),
        P(("row", "col"), None),
        P(("row", "col"), None),
        P("row", "col", None, None),
        P("row", "col", None, None, None, None),
    )
    return jax.shard_map(
        shards, mesh=mesh, in_specs=placed, out_specs=P(("row", "col"), None), check_vma=False
    )
```

```python
import jax
import jax.numpy as jnp
from jax import lax
from jax.experimental import pallas as pl
from jax.experimental.pallas import tpu as pltpu
from jax.sharding import PartitionSpec as P

MESH = pl.DeviceIdType.MESH
F32, BF16, I16, I32 = jnp.float32, jnp.bfloat16, jnp.int16, jnp.int32

ZS, XS, HI = 8, 4, 2
TILE, BAND, TILES = 128, 4, 16
LVLS = 3
NB = 2
PR = 80
QR = TILE - PR
ORDER = (0, 1, 2, 5, 6, 3, 4, 7)
FWD = (-5.0, 1365.0)
BWD = (-44.0, 744.0)
LN2 = 0.6931471805599453


def encode(x, code):
    low, steps = code
    v = jnp.log(jnp.maximum(x, 2.0**low)) * (steps / LN2) + (0.5 - low * steps)
    return (v.astype(I32) - 32768).astype(I16)


def decode(c, code):
    low, steps = code
    v = c.astype(I32).astype(F32)
    x = jnp.exp(v * (LN2 / steps) + (32768.0 / steps + low) * LN2)
    return jnp.where(v > -32768.0, x, 0.0)


def kernel(
    tsrc, bslot, paths_hbm, dep_hbm, levels_hbm, pattern, out,
    paths_in, dep_in, levels,
    stage, acat, at, gath, wgtp, wgtq, local, part, paths, total,
    ysend, yrecv, zsend, zrecv, qsend, qrecv, fsend, frecv, csend, crecv, isend, irecv,
    load_sem, in_sem,
    ag_s, ag_r, sib_s, sib_r, y_s, y_r, z_s, z_r, q_s, q_r, f_s, f_r,
    wz_s, wz_r, wy_s, wy_r, wq_s, wq_r, wf_s, wf_r, c_s, c_r, i_s, i_r,
):
    r, c = lax.axis_index("row"), lax.axis_index("col")
    z, y = r // 2, r % 2
    chip, core = c // 2, c % 2
    yhi, x = chip // XS, chip % XS
    lanes = gath.shape[-1]

    def load(i):
        return pltpu.make_async_copy(pattern.at[pl.ds(i * BAND, BAND)], stage.at[i], load_sem.at[i])

    inputs = [
        pltpu.make_async_copy(src, dst, in_sem.at[n])
        for n, (src, dst) in enumerate(
            [(paths_hbm, paths_in), (levels_hbm, levels), (dep_hbm, dep_in)]
        )
    ]
    for copy in inputs:
        copy.start()
    for i in range(TILES):
        load(i).start()

    def z_off(j):
        return (1 - 2 * core) * jnp.where(j % 2 == 1, (7 - j) // 2, -((8 - j) // 2))

    def z_to(j):
        return (z + z_off(j) + ZS) % ZS

    def c_to(n, sign=1):
        dx, dy = (7 - n) % XS, (7 - n) // XS
        return ((yhi + dy) % HI) * XS + (x + sign * dx + XS) % XS

    def z_dev(hops):
        return {"row": z_hop(hops) * 2 + y, "col": c}

    def z_hop(hops):
        return (z + (1 - 2 * core) * hops + ZS) % ZS

    def c_dev(n):
        return {"row": r, "col": c_to(n) * 2 + core}

    across = {"row": z * 2 + 1 - y, "col": c}
    sibling = {"row": r, "col": chip * 2 + 1 - core}

    def move(src, dst, ssem, rsem, dev):
        return pltpu.make_async_remote_copy(
            src_ref=src, dst_ref=dst, send_sem=ssem, recv_sem=rsem, device_id=dev, device_id_type=MESH
        )

    barrier = pltpu.get_barrier_semaphore()
    partners = [across, sibling] + [z_dev(hops) for hops in (2, 1, -1, -2)] + [c_dev(n) for n in range(7)]
    for dev in partners:
        pl.semaphore_signal(barrier, inc=1, device_id=dev, device_id_type=MESH)
    pl.semaphore_wait(barrier, len(partners))

    def ag_move(b, lvl, n, place):
        ref = gath.at[b, lvl, place]
        return move(ref, ref, ag_s.at[b, n], ag_r.at[b, lvl, n], c_dev(n))

    def sib_move(b, lvl, n):
        ref = gath.at[b, lvl, core * 8 + c_to(n, -1)]
        return move(ref, ref, sib_s.at[b, n], sib_r.at[b, lvl, n], sibling)

    def y_move(b, lvl, j):
        return move(ysend.at[b, j], yrecv.at[b, lvl, j], y_s.at[b, j], y_r.at[b, lvl, j], across)

    def hop_dev(j):
        return z_dev((2, 1, -1, 2, -2, 1, -1)[j])

    def z_move(b, lvl, j):
        return move(zsend.at[b, j], zrecv.at[b, lvl, j], z_s.at[b, j], z_r.at[b, lvl, j], hop_dev(j))

    def q_move(b, lvl, j):
        return move(qsend.at[b, j], qrecv.at[b, lvl, j], q_s.at[b, j], q_r.at[b, lvl, j], hop_dev(j))

    def f_move(b, lvl):
        return move(fsend.at[b, 0], frecv.at[b, lvl, 0], f_s.at[b, 0], f_r.at[b, lvl, 0], across)

    def y_sum(b, lvl, j):
        y_move(b, lvl, j).wait_recv()
        return part[b, 0, j, :PR] + decode(yrecv[b, lvl, j], FWD)

    def z_go(b, lvl, j):
        v = y_sum(b, lvl, j)
        for m in {3: (1, 0), 4: (2,)}.get(j, ()):
            z_move(b, lvl, m).wait_recv()
            v += decode(zrecv[b, lvl, m], FWD)
        zsend[b, j] = encode(v, FWD)
        z_move(b, lvl, j).start()

    def q_go(b, lvl, j):
        joined = {3: (1, 0), 4: (2,)}.get(j, ())
        for m in joined:
            q_move(b, lvl, m).wait_recv()
        for k in range(2):
            v = part[b, k, j, PR:]
            for m in joined:
                v += decode(qrecv[b, lvl, m, k], FWD)
            qsend[b, j, k] = encode(v, FWD)
        q_move(b, lvl, j).start()

    def fwd_send(b, lvl, value):
        gath[b, lvl, core * 8 + chip] = value.astype(BF16)
        for n in range(7):
            ag_move(b, lvl, n, core * 8 + chip).start()
        sib_move(b, lvl, 7).start()

    def fwd_pass(b, lvl):
        local[b, core * 8 + chip] = gath[b, lvl, core * 8 + chip]
        for n in (6, 4, 5, 3, 2, 0, 1):
            place = core * 8 + c_to(n, -1)
            ag_move(b, lvl, n, place).wait_recv()
            sib_move(b, lvl, n).start()
            local[b, place] = gath[b, lvl, place]

    def fwd_tile(b, i):
        rhs = jnp.concatenate([local[b, tsrc[e, i]] for e in range(BAND)], axis=0)
        return jnp.dot(acat[i], rhs, preferred_element_type=F32)

    def fwd_work(b, lvl):
        for n in (7, 6, 4, 5, 3, 2, 0, 1):
            sib_move(b, lvl, n).wait_recv()
            local[b, (1 - core) * 8 + c_to(n, -1)] = gath[b, lvl, (1 - core) * 8 + c_to(n, -1)]

        def pair(j):
            for k, i in ((1, z_to(j) * 2 + 1 - y), (0, z_to(j) * 2 + y)):
                part[b, k, j] = fwd_tile(b, i)
            if j < 3:
                q_go(b, lvl, j)
            ysend[b, j] = encode(part[b, 1, j, :PR], FWD)
            y_move(b, lvl, j).start()

        for j in ORDER:
            pair(j)
            if j == 6:
                q_go(b, lvl, 5)
                q_go(b, lvl, 6)

        for n in range(7):
            ag_move(b, lvl, n, chip).wait_send()
        for k in range(8):
            sib_move(b, lvl, k).wait_send()

    def fwd_far(b, lvl):
        for j in (0, 1, 2):
            z_go(b, lvl, j)

    def fwd_joined_late(b, lvl):
        for j in (3, 4):
            q_go(b, lvl, j)

    def fwd_near(b, lvl):
        for j in (5, 6):
            z_go(b, lvl, j)

    def fwd_joined(b, lvl):
        for j in (3, 4):
            z_go(b, lvl, j)

    def fwd_late(b, lvl):
        own = part[b, 0, 7, PR:]
        other = part[b, 1, 7, PR:]
        for j in (6, 5, 4, 3):
            q_move(b, lvl, j).wait_recv()
            own += decode(qrecv[b, lvl, j, 0], FWD)
            other += decode(qrecv[b, lvl, j, 1], FWD)
        fsend[b, 0] = encode(other, FWD)
        f_move(b, lvl).start()
        total[b, PR:] = own

    def fwd_end(b, lvl, go):
        mine = y_sum(b, lvl, 7)
        for j in (6, 5, 4, 3):
            z_move(b, lvl, j).wait_recv()
            mine += decode(zrecv[b, lvl, j], FWD)
        total[b, :PR] = mine
        f_move(b, lvl).wait()
        total[b, PR:] += decode(frecv[b, lvl, 0], FWD)
        level = lvl + 1
        value = jnp.where(levels_of(b) == level, total[b], 0.0)
        paths[b, level] = value
        go(value)
        for j in range(7):
            q_move(b, lvl, j).wait_send()
            z_move(b, lvl, j).wait_send()
        for j in range(8):
            y_move(b, lvl, j).wait_send()

    def relay_dev(j):
        return z_dev((2, -2, 1, -1, 2, 1, -1)[j])

    def origin(j):
        return z_hop((-2, 2, -1, 1, -4, -3, 3)[j])

    def slot_from(j):
        return {4: 1, 5: 1, 6: 2}.get(j, 0)

    def wz_move(b, lvl, j):
        src, dst = wgtp.at[b, lvl, 0, slot_from(j)], wgtp.at[b, lvl, 0, 1 + j]
        return move(src, dst, wz_s.at[b, j], wz_r.at[b, lvl, j], relay_dev(j))

    def wq_move(b, lvl, j):
        src, dst = wgtq.at[b, lvl, slot_from(j)], wgtq.at[b, lvl, 1 + j]
        return move(src, dst, wq_s.at[b, j], wq_r.at[b, lvl, j], relay_dev(j))

    def wy_move(b, lvl, g):
        src, dst = wgtp.at[b, lvl, 0, g], wgtp.at[b, lvl, 1, g]
        return move(src, dst, wy_s.at[b, g], wy_r.at[b, lvl, g], across)

    def wf_move(b, lvl):
        ref = wgtq.at[b, lvl, 0, y]
        return move(ref, ref, wf_s.at[b, 0], wf_r.at[b, lvl, 0], across)

    def c_move(b, lvl, n):
        return move(csend.at[b, n], crecv.at[b, lvl, n], c_s.at[b, n], c_r.at[b, lvl, n], sibling)

    def i_move(b, lvl, n):
        return move(isend.at[b, n], irecv.at[b, lvl, n], i_s.at[b, n], i_r.at[b, lvl, n], c_dev(n))

    def bwd_send(b, lvl, value):
        value = value.astype(BF16)
        wgtq[b, lvl, 0, y] = value[PR:]
        wf_move(b, lvl).start()
        wgtp[b, lvl, 0, 0] = value[:PR]
        for j in range(4):
            wz_move(b, lvl, j).start()
        wy_move(b, lvl, 0).start()

    def keep_p(b, lvl, side, slot):
        zz = origin(slot - 1) if slot else z
        local[b, zz * 2 + (1 - y if side else y), :PR] = wgtp[b, lvl, side, slot]

    def keep_q(b, lvl, slot):
        zz = origin(slot - 1) if slot else z
        local[b, pl.ds(zz * 2, 2), PR:] = wgtq[b, lvl, slot]

    def bwd_pass(b, lvl):
        wf_move(b, lvl).wait_recv()
        for j in range(4):
            wq_move(b, lvl, j).start()

    def bwd_near(b, lvl):
        for j in (2, 3, 0, 1):
            wz_move(b, lvl, j).wait_recv()
            for m in {0: (4, 5), 1: (6,)}.get(j, ()):
                wz_move(b, lvl, m).start()
            wy_move(b, lvl, 1 + j).start()

    def bwd_late(b, lvl):
        for j in (0, 1):
            wq_move(b, lvl, j).wait_recv()
            for m in {0: (4, 5), 1: (6,)}[j]:
                wq_move(b, lvl, m).start()
        for slot in range(5):
            keep_p(b, lvl, 0, slot)
        for slot in range(3):
            keep_q(b, lvl, slot)

    def bwd_far(b, lvl):
        for j in (5, 6, 4):
            wz_move(b, lvl, j).wait_recv()
            wy_move(b, lvl, 1 + j).start()
        for slot in range(5, 8):
            keep_p(b, lvl, 0, slot)

    def bwd_rest(b, lvl):
        for j in (2, 3, 5, 6, 4):
            wq_move(b, lvl, j).wait_recv()
            keep_q(b, lvl, 1 + j)

    def bwd_tile(b, t):
        slots = [bslot[t * BAND + e] for e in range(BAND)]
        lhs = jnp.concatenate([at[k] for k in slots], axis=1)
        rhs = jnp.concatenate([local[b, k % TILES] for k in slots], axis=0)
        return jnp.dot(lhs, rhs, preferred_element_type=F32)

    def bwd_work(b, lvl):
        for slot in (0, 3, 4, 1, 2, 6, 7, 5):
            wy_move(b, lvl, slot).wait_recv()
            keep_p(b, lvl, 1, slot)

        def sums(n):
            part[b, 0, n] = bwd_tile(b, c_to(n) * 2 + core)
            c_move(b, lvl, n).wait_recv()
            v = part[b, 0, n] + decode(crecv[b, lvl, n], BWD)
            if n == 7:
                total[b] = v
                return
            isend[b, n] = encode(v, BWD)
            i_move(b, lvl, n).start()

        ahead = 3
        for n in range(8 + ahead):
            if n < 8:
                csend[b, n] = encode(bwd_tile(b, c_to(n) * 2 + 1 - core), BWD)
                c_move(b, lvl, n).start()
            if n >= ahead:
                sums(n - ahead)
        for j in range(7):
            wz_move(b, lvl, j).wait_send()
            wq_move(b, lvl, j).wait_send()
        for g in range(8):
            wy_move(b, lvl, g).wait_send()
        wf_move(b, lvl).wait_send()

    def bwd_end(b, lvl, go):
        level = 2 - lvl
        for n in (6, 4, 5, 3, 2, 0, 1):
            i_move(b, lvl, n).wait_recv()
            total[b] += decode(irecv[b, lvl, n], BWD)
        mask = levels_of(b) == level
        counts = paths[b, level]
        delta = jnp.where(mask, counts * total[b], 0.0)
        go(jnp.where(mask, 1.0 + delta, 0.0) / jnp.maximum(counts, 1.0))
        out[:, b * lanes : (b + 1) * lanes] += delta
        for n in range(7):
            i_move(b, lvl, n).wait_send()
        for n in range(8):
            c_move(b, lvl, n).wait_send()

    def levels_of(b):
        return levels[:, b * lanes : (b + 1) * lanes]

    def fwd_next(b, lvl):
        def go(value):
            @pl.when(lvl < LVLS - 1)
            def _():
                fwd_send(b, lvl + 1, value)

            @pl.when(lvl == LVLS - 1)
            def _():
                top = 1.0 + dep_in[:, b * lanes : (b + 1) * lanes]
                bwd_send(b, 0, jnp.where(levels_of(b) == 3, top, 0.0) / jnp.maximum(value, 1.0))

        fwd_end(b, lvl, go)

    def bwd_next(b, lvl):
        def go(value):
            @pl.when(lvl < LVLS - 1)
            def _():
                bwd_send(b, lvl + 1, value)

        bwd_end(b, lvl, go)

    inputs[0].wait()
    inputs[1].wait()
    for b in range(NB):
        value = jnp.where(levels_of(b) == 0, paths_in[:, b * lanes : (b + 1) * lanes], 0.0)
        paths[b, 0] = value
        fwd_send(b, 0, value)
    inputs[2].wait()
    out[...] = jnp.zeros_like(out)

    eye = (
        lax.broadcasted_iota(I32, (TILE, TILE), 0) == lax.broadcasted_iota(I32, (TILE, TILE), 1)
    ).astype(F32).astype(BF16)
    for i in range(TILES):
        load(i).wait()

    @pl.loop(0, TILES)
    def _(i):
        for e in range(BAND):
            tile = stage[i, e].astype(F32).astype(BF16)
            acat[i, :, e * TILE : (e + 1) * TILE] = tile
            at[e * TILES + i] = lax.dot_general(
                eye, tile, (((1,), (1,)), ((), ())), preferred_element_type=F32
            ).astype(BF16)

    batches = range(NB)

    def each(*stages):
        def body(lvl):
            for stage in stages:
                for b in batches:
                    stage(b, lvl)

        return body

    pl.loop(0, LVLS)(each(fwd_pass, fwd_work, fwd_far, fwd_joined_late, fwd_near, fwd_joined, fwd_late, fwd_next))
    pl.loop(0, LVLS)(each(bwd_pass, bwd_near, bwd_late, bwd_far, bwd_rest, bwd_work, bwd_next))


def slots_by_source(flat):
    slots = jnp.arange(TILES * BAND, dtype=I32)
    same = (flat[:, None] == flat[None, :]) & (slots[:, None] < slots[None, :])
    before = jnp.sum(same.astype(I32), axis=0)
    mine = flat[None, :] == jnp.arange(TILES, dtype=I32)[:, None]
    nth = before[None, :] == jnp.arange(BAND, dtype=I32)[:, None]
    picked = mine[:, None, :] & nth[None, :, :]
    return jnp.sum(jnp.where(picked, slots, 0), axis=2).reshape(-1)


def shards(paths_in, dep_in, levels, tile_src, pattern):
    rows, sources = paths_in.shape
    by_slot = tile_src[0, 0].T
    back = slots_by_source(by_slot.reshape(-1))
    by_slot = by_slot % 2 * 8 + by_slot // 2
    pattern = pattern.reshape(TILES * BAND, TILE, TILE)
    vmem, smem, hbm = (
        pl.BlockSpec(memory_space=m) for m in (pltpu.VMEM, pltpu.SMEM, pltpu.HBM)
    )
    block = (rows, sources // NB)
    whole = (rows, sources)

    def dma(*shape):
        return pltpu.SemaphoreType.DMA(shape)

    def pairs(*counts):
        return [d for n in counts for d in (dma(NB, n), dma(NB, LVLS, n))]

    def slots(*dims):
        shape = (*dims, sources // NB)
        return [pltpu.VMEM((NB, *shape), I16), pltpu.VMEM((NB, LVLS, *shape), I16)]

    return pl.pallas_call(
        kernel,
        out_shape=jax.ShapeDtypeStruct(whole, F32),
        in_specs=[smem, smem, hbm, hbm, hbm, hbm],
        out_specs=vmem,
        scratch_shapes=[
            pltpu.VMEM(whole, F32),
            pltpu.VMEM(whole, F32),
            pltpu.VMEM(whole, I32),
            pltpu.VMEM((TILES, BAND, TILE, TILE), I32),
            pltpu.VMEM((TILES, TILE, BAND * TILE), BF16),
            pltpu.VMEM((TILES * BAND, TILE, TILE), BF16),
            pltpu.VMEM((NB, LVLS, TILES, *block), BF16),
            pltpu.VMEM((NB, LVLS, 2, 8, PR, block[1]), BF16),
            pltpu.VMEM((NB, LVLS, 8, 2, QR, block[1]), BF16),
            pltpu.VMEM((NB, TILES, *block), BF16),
            pltpu.VMEM((NB, 2, 8, *block), F32),
            pltpu.VMEM((NB, 4, *block), F32),
            pltpu.VMEM((NB, *block), F32),
            *slots(8, PR), *slots(7, PR), *slots(7, 2, QR), *slots(1, QR), *slots(8, rows), *slots(7, rows),
            dma(TILES),
            dma(3),
            *pairs(7, 8, 8, 7, 7, 1),
            *pairs(7, 8, 7, 1, 8, 7),
        ],
        compiler_params=pltpu.CompilerParams(
            collective_id=0, has_side_effects=True, vmem_limit_bytes=56 * 1024 * 1024
        ),
    )(by_slot, back, paths_in, dep_in, levels, pattern)


def solution(mesh):
    placed = (
        P(("row", "col"), None),
        P(("row", "col"), None),
        P(("row", "col"), None),
        P("row", "col", None, None),
        P("row", "col", None, None, None, None),
    )
    return jax.shard_map(
        shards, mesh=mesh, in_specs=placed, out_specs=P(("row", "col"), None), check_vma=False
    )
```

```python
import jax
import jax.numpy as jnp
from jax import lax
from jax.experimental import pallas as pl
from jax.experimental.pallas import tpu as pltpu
from jax.sharding import PartitionSpec as P

MESH = pl.DeviceIdType.MESH
F32, BF16, I16, I32 = jnp.float32, jnp.bfloat16, jnp.int16, jnp.int32

ZS, XS, HI = 8, 4, 2
TILE, BAND, TILES = 128, 4, 16
LVLS = 3
NB = 2
PR = 80
QR = TILE - PR
ORDER = (0, 1, 2, 5, 6, 3, 4, 7)
FWD = (-5.0, 1365.0)
BWD = (-44.0, 744.0)
LN2 = 0.6931471805599453


def encode(x, code):
    low, steps = code
    v = jnp.log(jnp.maximum(x, 2.0**low)) * (steps / LN2) + (0.5 - low * steps)
    return (v.astype(I32) - 32768).astype(I16)


def decode(c, code):
    low, steps = code
    v = c.astype(I32).astype(F32)
    x = jnp.exp(v * (LN2 / steps) + (32768.0 / steps + low) * LN2)
    return jnp.where(v > -32768.0, x, 0.0)


def kernel(
    tsrc, bslot, paths_hbm, dep_hbm, levels_hbm, pattern, out,
    paths_in, dep_in, levels,
    stage, acat, at, gath, wgtp, wgtq, local, part, paths, total,
    ysend, yrecv, zsend, zrecv, qsend, qrecv, fsend, frecv, csend, crecv, isend, irecv,
    load_sem, in_sem,
    ag_s, ag_r, sib_s, sib_r, y_s, y_r, z_s, z_r, q_s, q_r, f_s, f_r,
    wz_s, wz_r, wy_s, wy_r, wq_s, wq_r, wf_s, wf_r, c_s, c_r, i_s, i_r,
):
    r, c = lax.axis_index("row"), lax.axis_index("col")
    z, y = r // 2, r % 2
    chip, core = c // 2, c % 2
    yhi, x = chip // XS, chip % XS
    lanes = gath.shape[-1]

    def load(i):
        return pltpu.make_async_copy(pattern.at[pl.ds(i * BAND, BAND)], stage.at[i], load_sem.at[i])

    inputs = [
        pltpu.make_async_copy(src, dst, in_sem.at[n])
        for n, (src, dst) in enumerate(
            [(paths_hbm, paths_in), (levels_hbm, levels), (dep_hbm, dep_in)]
        )
    ]
    for copy in inputs:
        copy.start()
    for i in range(TILES):
        load(i).start()

    def z_off(j):
        return (1 - 2 * core) * jnp.where(j % 2 == 1, (7 - j) // 2, -((8 - j) // 2))

    def z_to(j):
        return (z + z_off(j) + ZS) % ZS

    def c_to(n, sign=1):
        dx, dy = (7 - n) % XS, (7 - n) // XS
        return ((yhi + dy) % HI) * XS + (x + sign * dx + XS) % XS

    def z_dev(hops):
        return {"row": z_hop(hops) * 2 + y, "col": c}

    def z_hop(hops):
        return (z + (1 - 2 * core) * hops + ZS) % ZS

    def c_dev(n):
        return {"row": r, "col": c_to(n) * 2 + core}

    across = {"row": z * 2 + 1 - y, "col": c}
    sibling = {"row": r, "col": chip * 2 + 1 - core}

    def move(src, dst, ssem, rsem, dev):
        return pltpu.make_async_remote_copy(
            src_ref=src, dst_ref=dst, send_sem=ssem, recv_sem=rsem, device_id=dev, device_id_type=MESH
        )

    barrier = pltpu.get_barrier_semaphore()
    partners = [across, sibling] + [z_dev(hops) for hops in (2, 1, -1, -2)] + [c_dev(n) for n in range(7)]
    for dev in partners:
        pl.semaphore_signal(barrier, inc=1, device_id=dev, device_id_type=MESH)
    pl.semaphore_wait(barrier, len(partners))

    def ag_move(b, lvl, n, place):
        ref = gath.at[b, lvl, place]
        return move(ref, ref, ag_s.at[b, n], ag_r.at[b, lvl, n], c_dev(n))

    def sib_move(b, lvl, n):
        ref = gath.at[b, lvl, core * 8 + c_to(n, -1)]
        return move(ref, ref, sib_s.at[b, n], sib_r.at[b, lvl, n], sibling)

    def y_move(b, lvl, j):
        return move(ysend.at[b, j], yrecv.at[b, lvl, j], y_s.at[b, j], y_r.at[b, lvl, j], across)

    def hop_dev(j):
        return z_dev((2, 1, -1, 2, -2, 1, -1)[j])

    def z_move(b, lvl, j):
        return move(zsend.at[b, j], zrecv.at[b, lvl, j], z_s.at[b, j], z_r.at[b, lvl, j], hop_dev(j))

    def q_move(b, lvl, j):
        return move(qsend.at[b, j], qrecv.at[b, lvl, j], q_s.at[b, j], q_r.at[b, lvl, j], hop_dev(j))

    def f_move(b, lvl):
        return move(fsend.at[b, 0], frecv.at[b, lvl, 0], f_s.at[b, 0], f_r.at[b, lvl, 0], across)

    def y_sum(b, lvl, j):
        y_move(b, lvl, j).wait_recv()
        return part[b, 0, j, :PR] + decode(yrecv[b, lvl, j], FWD)

    def z_go(b, lvl, j):
        v = y_sum(b, lvl, j)
        for m in {3: (1, 0), 4: (2,)}.get(j, ()):
            z_move(b, lvl, m).wait_recv()
            v += decode(zrecv[b, lvl, m], FWD)
        zsend[b, j] = encode(v, FWD)
        z_move(b, lvl, j).start()

    def q_go(b, lvl, j):
        joined = {3: (1, 0), 4: (2,)}.get(j, ())
        for m in joined:
            q_move(b, lvl, m).wait_recv()
        for k in range(2):
            v = part[b, k, j, PR:]
            for m in joined:
                v += decode(qrecv[b, lvl, m, k], FWD)
            qsend[b, j, k] = encode(v, FWD)
        q_move(b, lvl, j).start()

    def fwd_send(b, lvl, value):
        gath[b, lvl, core * 8 + chip] = value.astype(BF16)
        for n in range(7):
            ag_move(b, lvl, n, core * 8 + chip).start()
        sib_move(b, lvl, 7).start()

    def fwd_pass(b, lvl):
        local[b, core * 8 + chip] = gath[b, lvl, core * 8 + chip]
        for n in (6, 4, 5, 3, 2, 0, 1):
            place = core * 8 + c_to(n, -1)
            ag_move(b, lvl, n, place).wait_recv()
            sib_move(b, lvl, n).start()
            local[b, place] = gath[b, lvl, place]

    def fwd_tile(b, i):
        rhs = jnp.concatenate([local[b, tsrc[e, i]] for e in range(BAND)], axis=0)
        return jnp.dot(acat[i], rhs, preferred_element_type=F32)

    def fwd_work(b, lvl):
        for n in (7, 6, 4, 5, 3, 2, 0, 1):
            sib_move(b, lvl, n).wait_recv()
            local[b, (1 - core) * 8 + c_to(n, -1)] = gath[b, lvl, (1 - core) * 8 + c_to(n, -1)]

        def pair(j):
            for k, i in ((1, z_to(j) * 2 + 1 - y), (0, z_to(j) * 2 + y)):
                part[b, k, j] = fwd_tile(b, i)
            if j < 3:
                q_go(b, lvl, j)
            ysend[b, j] = encode(part[b, 1, j, :PR], FWD)
            y_move(b, lvl, j).start()

        for j in ORDER:
            pair(j)
            if j == 6:
                q_go(b, lvl, 5)
                q_go(b, lvl, 6)

        for n in range(7):
            ag_move(b, lvl, n, chip).wait_send()
        for k in range(8):
            sib_move(b, lvl, k).wait_send()

    def fwd_far(b, lvl):
        for j in (0, 1, 2):
            z_go(b, lvl, j)

    def fwd_joined_late(b, lvl):
        for j in (3, 4):
            q_go(b, lvl, j)

    def fwd_near(b, lvl):
        for j in (5, 6):
            z_go(b, lvl, j)

    def fwd_joined(b, lvl):
        for j in (3, 4):
            z_go(b, lvl, j)

    def fwd_late(b, lvl):
        own = part[b, 0, 7, PR:]
        other = part[b, 1, 7, PR:]
        for j in (6, 5, 4, 3):
            q_move(b, lvl, j).wait_recv()
            own += decode(qrecv[b, lvl, j, 0], FWD)
            other += decode(qrecv[b, lvl, j, 1], FWD)
        fsend[b, 0] = encode(other, FWD)
        f_move(b, lvl).start()
        total[b, PR:] = own

    def fwd_end(b, lvl, go):
        mine = y_sum(b, lvl, 7)
        for j in (6, 5, 4, 3):
            z_move(b, lvl, j).wait_recv()
            mine += decode(zrecv[b, lvl, j], FWD)
        total[b, :PR] = mine
        f_move(b, lvl).wait()
        total[b, PR:] += decode(frecv[b, lvl, 0], FWD)
        level = lvl + 1
        value = jnp.where(levels_of(b) == level, total[b], 0.0)
        paths[b, level] = value
        go(value)
        for j in range(7):
            q_move(b, lvl, j).wait_send()
            z_move(b, lvl, j).wait_send()
        for j in range(8):
            y_move(b, lvl, j).wait_send()

    def relay_dev(j):
        return z_dev((2, -2, 1, -1, 2, 1, -1)[j])

    def origin(j):
        return z_hop((-2, 2, -1, 1, -4, -3, 3)[j])

    def slot_from(j):
        return {4: 1, 5: 1, 6: 2}.get(j, 0)

    def wz_move(b, lvl, j):
        src, dst = wgtp.at[b, lvl, 0, slot_from(j)], wgtp.at[b, lvl, 0, 1 + j]
        return move(src, dst, wz_s.at[b, j], wz_r.at[b, lvl, j], relay_dev(j))

    def wq_move(b, lvl, j):
        src, dst = wgtq.at[b, lvl, slot_from(j)], wgtq.at[b, lvl, 1 + j]
        return move(src, dst, wq_s.at[b, j], wq_r.at[b, lvl, j], relay_dev(j))

    def wy_move(b, lvl, g):
        src, dst = wgtp.at[b, lvl, 0, g], wgtp.at[b, lvl, 1, g]
        return move(src, dst, wy_s.at[b, g], wy_r.at[b, lvl, g], across)

    def wf_move(b, lvl):
        ref = wgtq.at[b, lvl, 0, y]
        return move(ref, ref, wf_s.at[b, 0], wf_r.at[b, lvl, 0], across)

    def c_move(b, lvl, n):
        return move(csend.at[b, n], crecv.at[b, lvl, n], c_s.at[b, n], c_r.at[b, lvl, n], sibling)

    def i_move(b, lvl, n):
        return move(isend.at[b, n], irecv.at[b, lvl, n], i_s.at[b, n], i_r.at[b, lvl, n], c_dev(n))

    def bwd_send(b, lvl, value):
        value = value.astype(BF16)
        wgtq[b, lvl, 0, y] = value[PR:]
        wf_move(b, lvl).start()
        wgtp[b, lvl, 0, 0] = value[:PR]
        for j in range(4):
            wz_move(b, lvl, j).start()
        wy_move(b, lvl, 0).start()

    def keep_p(b, lvl, side, slot):
        zz = origin(slot - 1) if slot else z
        local[b, zz * 2 + (1 - y if side else y), :PR] = wgtp[b, lvl, side, slot]

    def keep_q(b, lvl, slot):
        zz = origin(slot - 1) if slot else z
        local[b, pl.ds(zz * 2, 2), PR:] = wgtq[b, lvl, slot]

    def bwd_pass(b, lvl):
        wf_move(b, lvl).wait_recv()
        for j in range(4):
            wq_move(b, lvl, j).start()

    def bwd_near(b, lvl):
        for j in (2, 3, 0, 1):
            wz_move(b, lvl, j).wait_recv()
            for m in {0: (4, 5), 1: (6,)}.get(j, ()):
                wz_move(b, lvl, m).start()
            wy_move(b, lvl, 1 + j).start()

    def bwd_late(b, lvl):
        for j in (0, 1):
            wq_move(b, lvl, j).wait_recv()
            for m in {0: (4, 5), 1: (6,)}[j]:
                wq_move(b, lvl, m).start()
        for slot in range(5):
            keep_p(b, lvl, 0, slot)
        for slot in range(3):
            keep_q(b, lvl, slot)

    def bwd_far(b, lvl):
        for j in (5, 6, 4):
            wz_move(b, lvl, j).wait_recv()
            wy_move(b, lvl, 1 + j).start()
        for slot in range(5, 8):
            keep_p(b, lvl, 0, slot)

    def bwd_rest(b, lvl):
        for j in (2, 3, 5, 6, 4):
            wq_move(b, lvl, j).wait_recv()
            keep_q(b, lvl, 1 + j)

    def bwd_tile(b, t):
        slots = [bslot[t * BAND + e] for e in range(BAND)]
        lhs = jnp.concatenate([at[k] for k in slots], axis=1)
        rhs = jnp.concatenate([local[b, k % TILES] for k in slots], axis=0)
        return jnp.dot(lhs, rhs, preferred_element_type=F32)

    def bwd_work(b, lvl):
        for slot in (0, 3, 4, 1, 2, 6, 7, 5):
            wy_move(b, lvl, slot).wait_recv()
            keep_p(b, lvl, 1, slot)

        def sums(n):
            part[b, 0, n] = bwd_tile(b, c_to(n) * 2 + core)
            c_move(b, lvl, n).wait_recv()
            v = part[b, 0, n] + decode(crecv[b, lvl, n], BWD)
            if n == 7:
                total[b] = v
                return
            isend[b, n] = encode(v, BWD)
            i_move(b, lvl, n).start()

        ahead = 3
        for n in range(8 + ahead):
            if n < 8:
                csend[b, n] = encode(bwd_tile(b, c_to(n) * 2 + 1 - core), BWD)
                c_move(b, lvl, n).start()
            if n >= ahead:
                sums(n - ahead)
        for j in range(7):
            wz_move(b, lvl, j).wait_send()
            wq_move(b, lvl, j).wait_send()
        for g in range(8):
            wy_move(b, lvl, g).wait_send()
        wf_move(b, lvl).wait_send()

    def bwd_end(b, lvl, go):
        level = 2 - lvl
        for n in (6, 4, 5, 3, 2, 0, 1):
            i_move(b, lvl, n).wait_recv()
            total[b] += decode(irecv[b, lvl, n], BWD)
        mask = levels_of(b) == level
        counts = paths[b, level]
        delta = jnp.where(mask, counts * total[b], 0.0)
        go(jnp.where(mask, 1.0 + delta, 0.0) / jnp.maximum(counts, 1.0))
        out[:, b * lanes : (b + 1) * lanes] += delta
        for n in range(7):
            i_move(b, lvl, n).wait_send()
        for n in range(8):
            c_move(b, lvl, n).wait_send()

    def levels_of(b):
        return levels[:, b * lanes : (b + 1) * lanes]

    def fwd_next(b, lvl):
        def go(value):
            @pl.when(lvl < LVLS - 1)
            def _():
                fwd_send(b, lvl + 1, value)

            @pl.when(lvl == LVLS - 1)
            def _():
                top = 1.0 + dep_in[:, b * lanes : (b + 1) * lanes]
                bwd_send(b, 0, jnp.where(levels_of(b) == 3, top, 0.0) / jnp.maximum(value, 1.0))

        fwd_end(b, lvl, go)

    def bwd_next(b, lvl):
        def go(value):
            @pl.when(lvl < LVLS - 1)
            def _():
                bwd_send(b, lvl + 1, value)

        bwd_end(b, lvl, go)

    inputs[0].wait()
    inputs[1].wait()
    for b in range(NB):
        value = jnp.where(levels_of(b) == 0, paths_in[:, b * lanes : (b + 1) * lanes], 0.0)
        paths[b, 0] = value
        fwd_send(b, 0, value)
    inputs[2].wait()
    out[...] = jnp.zeros_like(out)

    eye = (
        lax.broadcasted_iota(I32, (TILE, TILE), 0) == lax.broadcasted_iota(I32, (TILE, TILE), 1)
    ).astype(F32).astype(BF16)
    for i in range(TILES):
        load(i).wait()

    @pl.loop(0, TILES)
    def _(i):
        for e in range(BAND):
            tile = stage[i, e].astype(F32).astype(BF16)
            acat[i, :, e * TILE : (e + 1) * TILE] = tile

    def transpose_half(lvl):
        @pl.loop(0, TILES // 2)
        def _(k):
            i = (lvl - 1) * (TILES // 2) + k
            for e in range(BAND):
                tile = acat[i, :, e * TILE : (e + 1) * TILE]
                at[e * TILES + i] = lax.dot_general(
                    eye, tile, (((1,), (1,)), ((), ())), preferred_element_type=F32
                ).astype(BF16)

    batches = range(NB)

    def each(*stages):
        def body(lvl):
            for stage in stages:
                for b in batches:
                    stage(b, lvl)

        return body

    def fwd_turn(b, lvl):
        if b == 0:
            pl.when(lvl > 0)(lambda: transpose_half(lvl))

    pl.loop(0, LVLS)(each(fwd_turn, fwd_pass, fwd_work, fwd_far, fwd_joined_late, fwd_near, fwd_joined, fwd_late, fwd_next))
    pl.loop(0, LVLS)(each(bwd_pass, bwd_near, bwd_late, bwd_far, bwd_rest, bwd_work, bwd_next))


def slots_by_source(flat):
    slots = jnp.arange(TILES * BAND, dtype=I32)
    same = (flat[:, None] == flat[None, :]) & (slots[:, None] < slots[None, :])
    before = jnp.sum(same.astype(I32), axis=0)
    mine = flat[None, :] == jnp.arange(TILES, dtype=I32)[:, None]
    nth = before[None, :] == jnp.arange(BAND, dtype=I32)[:, None]
    picked = mine[:, None, :] & nth[None, :, :]
    return jnp.sum(jnp.where(picked, slots, 0), axis=2).reshape(-1)


def shards(paths_in, dep_in, levels, tile_src, pattern):
    rows, sources = paths_in.shape
    by_slot = tile_src[0, 0].T
    back = slots_by_source(by_slot.reshape(-1))
    by_slot = by_slot % 2 * 8 + by_slot // 2
    pattern = pattern.reshape(TILES * BAND, TILE, TILE)
    vmem, smem, hbm = (
        pl.BlockSpec(memory_space=m) for m in (pltpu.VMEM, pltpu.SMEM, pltpu.HBM)
    )
    block = (rows, sources // NB)
    whole = (rows, sources)

    def dma(*shape):
        return pltpu.SemaphoreType.DMA(shape)

    def pairs(*counts):
        return [d for n in counts for d in (dma(NB, n), dma(NB, LVLS, n))]

    def slots(*dims):
        shape = (*dims, sources // NB)
        return [pltpu.VMEM((NB, *shape), I16), pltpu.VMEM((NB, LVLS, *shape), I16)]

    return pl.pallas_call(
        kernel,
        out_shape=jax.ShapeDtypeStruct(whole, F32),
        in_specs=[smem, smem, hbm, hbm, hbm, hbm],
        out_specs=vmem,
        scratch_shapes=[
            pltpu.VMEM(whole, F32),
            pltpu.VMEM(whole, F32),
            pltpu.VMEM(whole, I32),
            pltpu.VMEM((TILES, BAND, TILE, TILE), I32),
            pltpu.VMEM((TILES, TILE, BAND * TILE), BF16),
            pltpu.VMEM((TILES * BAND, TILE, TILE), BF16),
            pltpu.VMEM((NB, LVLS, TILES, *block), BF16),
            pltpu.VMEM((NB, LVLS, 2, 8, PR, block[1]), BF16),
            pltpu.VMEM((NB, LVLS, 8, 2, QR, block[1]), BF16),
            pltpu.VMEM((NB, TILES, *block), BF16),
            pltpu.VMEM((NB, 2, 8, *block), F32),
            pltpu.VMEM((NB, 4, *block), F32),
            pltpu.VMEM((NB, *block), F32),
            *slots(8, PR), *slots(7, PR), *slots(7, 2, QR), *slots(1, QR), *slots(8, rows), *slots(7, rows),
            dma(TILES),
            dma(3),
            *pairs(7, 8, 8, 7, 7, 1),
            *pairs(7, 8, 7, 1, 8, 7),
        ],
        compiler_params=pltpu.CompilerParams(
            collective_id=0, has_side_effects=True, vmem_limit_bytes=56 * 1024 * 1024
        ),
    )(by_slot, back, paths_in, dep_in, levels, pattern)


def solution(mesh):
    placed = (
        P(("row", "col"), None),
        P(("row", "col"), None),
        P(("row", "col"), None),
        P("row", "col", None, None),
        P("row", "col", None, None, None, None),
    )
    return jax.shard_map(
        shards, mesh=mesh, in_specs=placed, out_specs=P(("row", "col"), None), check_vma=False
    )
```
